128 devices in a mesh: region: 8 (over y, core), tile: 16 (over z, x).
Axes of the slice: x: 4, y: 4, z: 4, core: 2. Of those that a mesh axis runs over, the one named last changes fastest.
Arguments:
- coeffs: float32 [4, 2048, 2048], P(None, 'tile', 'region')
- obs_cell: int32 [131072], P(('region', 'tile')), may hold values from 0 to 524287
- obs_value: float32 [8, 131072], P(None, ('region', 'tile')), may hold values from -6 to 6
- obs_count: int32 [128], P(('region', 'tile')), may hold values from 1 to 1024, 81920 in all
Outputs:
- solution_field: float32 [2048, 8, 2048], P('tile', None, 'region')
- residual: float32 [2048, 8, 2048], P('tile', None, 'region')
The draws below stay inside these ranges and needn't reach their ends.
Inputs may be any that keep to these rules, and one draw needn't show every extreme that they name: `obs_cell`: cell number y * 256 + x within the owning region's 2048 x 256 cells. `obs_count`: live slots stand at the head of each device's block; some device has all 1024 live.
All inputs are finite; a program needn't handle non-finite values.
Results may differ from the reference program's by a relative error of at most 0.00029.
Values sent between devices are 32-bit elements; how exact they have to be, the bound alone decides.
No kernel may reach another device: no remote copies, remote signals or barrier semaphores. Data moves between devices by JAX's collectives and lax.ppermute only.
A program may use at most 128 MiB of HBM per device.

```python
import math
import jax
import jax.numpy as jnp
import numpy as np

CX = 256
REALS = 8
ITERS = 2
OBS_DEV = 1024
NX = 2048
NY = 2048
OBS = 131072
REGION_CELLS = 524288
N_REGION = 8
N_TILE = 16


def draw_coeffs(key, part):
    keys = jax.random.split(jax.random.fold_in(key, 17), 4)
    shape = (NY, NX)
    along_x = jnp.exp(jax.random.uniform(keys[0], shape, jnp.float32, jnp.log(0.5), jnp.log(4.0)))
    along_y = jnp.exp(jax.random.uniform(keys[1], shape, jnp.float32, jnp.log(0.5), jnp.log(4.0)))
    mixed = jax.random.uniform(keys[2], shape, jnp.float32, -0.4, 0.4)
    reaction = jnp.exp(jax.random.uniform(keys[3], shape, jnp.float32, 0.0, jnp.log(4.0)))
    return jnp.stack([along_x, along_y, mixed, reaction], axis=0).astype(jnp.float32)


def plant(values, stream_key, smallest, largest):
    longest = values.shape.index(max(values.shape))
    spots = []
    for shift in (0, 1):
        where = [jax.random.randint(jax.random.fold_in(stream_key, axis), (), 0, length) for axis, length in enumerate(values.shape)]
        where[longest] = (where[longest] + shift) % values.shape[longest]
        spots.append(tuple(where))
    return values.at[spots[0]].set(smallest).at[spots[1]].set(largest)


def block_levels(own_key, dims, pieces, least, top_value):
    gain, own = 1.0, jax.random.fold_in(own_key, 6)
    for dim, blocks in pieces:
        steps = jnp.exp(jax.random.uniform(jax.random.fold_in(own, dim), (blocks,), jnp.float32, least / len(pieces), top_value / len(pieces)))
        gain = gain * jnp.repeat(steps, dims[dim] // blocks).reshape([-1 if axis == dim else 1 for axis in range(len(dims))])
    return gain


def split_up(amount, total, bound, slope):
    portions = [(1 << 20) // math.isqrt(rank ** slope) + 1 for rank in range(2, amount + 1)]
    spare, holding = total - bound - (amount - 1), [1] * (amount - 1)
    while spare > 0:
        movable = [i for i in range(amount - 1) if holding[i] < bound]
        pool, budget = sum([portions[i] for i in movable]), spare
        for i in movable:
            extra = min(bound - holding[i], max(1, budget * portions[i] // pool), spare)
            holding[i] = holding[i] + extra
            spare = spare - extra
    return np.array([bound] + holding)


def uneven_parts(rng, amount, total, limit, slope):
    if amount == 2:
        one = jax.random.randint(rng, (), max(1, total - limit), min(limit, total - 1) + 1)
        return jnp.stack([one, total - one])
    tallies = jnp.asarray(split_up(amount, total, limit, slope), jnp.int32)
    twos = (amount - 1) // 2
    source_of, taker = tallies[1:1 + 2 * twos:2], tallies[2:2 + 2 * twos:2]
    margin = jnp.minimum(source_of - 1, limit - taker)
    passed = jax.random.randint(jax.random.fold_in(rng, 1), (twos,), 0, 1 << 20) % (margin + 1)
    tallies = tallies.at[1:1 + 2 * twos:2].set(source_of - passed).at[2:2 + 2 * twos:2].set(taker + passed)
    return tallies[jax.random.permutation(jax.random.fold_in(rng, 2), amount)]


def normal_values(key, extent, deviation, limit, cuts=(), kind=jnp.bfloat16):
    array = deviation * jax.random.normal(key, extent, jnp.float32)
    if cuts:
        array = array * block_levels(key, extent, cuts, -0.22, 0.18)
    return jnp.clip(array, -limit, limit).astype(kind)


def setup_inputs(seed: int = 0) -> dict:
    splits = jax.random.split(jax.random.key(seed), 5)
    return {
        "coeffs": draw_coeffs(jax.random.fold_in(splits[4], 71), 0),
        "obs_cell": plant(jax.random.randint(splits[1], (OBS,), 0, REGION_CELLS), jax.random.fold_in(splits[1], 1), 0, REGION_CELLS - 1).astype(jnp.int32),
        "obs_value": normal_values(splits[2], (REALS, OBS), 1.0, 6.0, ((1, 128),), jnp.float32),
        "obs_count": uneven_parts(splits[3], N_REGION * N_TILE, OBS * 5 // 8, OBS_DEV, 2).astype(jnp.int32),
    }


noise_var = 0.5
prec_scale = 0.01


def stencil(padded, coef):
    along_x = coef[0]
    along_y = coef[1]
    mixed = coef[2]
    reaction = coef[3]
    centre = padded[1:-1, :, 1:-1]
    east_cell = padded[1:-1, :, 2:]
    west_cell = padded[1:-1, :, :-2]
    north_cell = padded[2:, :, 1:-1]
    south_cell = padded[:-2, :, 1:-1]
    north_east = padded[2:, :, 2:]
    north_west = padded[2:, :, :-2]
    south_east = padded[:-2, :, 2:]
    south_west = padded[:-2, :, :-2]
    middle_x = along_x[1:-1, 1:-1]
    middle_y = along_y[1:-1, 1:-1]
    east_face = (0.5 * (along_x[1:-1, 2:] + middle_x))[:, None, :]
    west_face = (0.5 * (along_x[1:-1, :-2] + middle_x))[:, None, :]
    north_face = (0.5 * (along_y[2:, 1:-1] + middle_y))[:, None, :]
    south_face = (0.5 * (along_y[:-2, 1:-1] + middle_y))[:, None, :]
    diffusion = east_face * (east_cell - centre) - west_face * (centre - west_cell)
    diffusion = diffusion + north_face * (north_cell - centre) - south_face * (centre - south_cell)
    cross_term = mixed[1:-1, 2:][:, None, :] * (north_east - south_east) - mixed[1:-1, :-2][:, None, :] * (north_west - south_west)
    cross_term = cross_term + mixed[2:, 1:-1][:, None, :] * (north_east - north_west) - mixed[:-2, 1:-1][:, None, :] * (south_east - south_west)
    return reaction[1:-1, 1:-1][:, None, :] * centre - diffusion - 0.25 * cross_term


def apply_k(field, coef_pad):
    padded = jnp.pad(field, ((1, 1), (0, 0), (1, 1)))
    return stencil(padded, coef_pad)


def reference(coeffs, obs_cell, obs_value, obs_count):
    slots = jnp.arange(OBS, dtype=jnp.int32)
    device = (slots // OBS_DEV).astype(jnp.int32)
    region = (device // N_TILE).astype(jnp.int32)
    live = (slots % OBS_DEV) < obs_count[device]
    row_y = obs_cell // CX
    column = region * CX + obs_cell % CX
    flat = (row_y * NX + column).astype(jnp.int32)
    weight = jnp.where(live, 1.0, 0.0).astype(jnp.float32)
    counts = jnp.zeros((NY * NX,), jnp.float32).at[flat].add(weight)
    data = jnp.zeros((REALS, NY * NX), jnp.float32).at[:, flat].add(obs_value * weight[None, :])
    right_side = jnp.transpose(data.reshape(REALS, NY, NX), (1, 0, 2)) / noise_var
    obs_weight = (counts.reshape(NY, NX) / noise_var)[:, None, :]
    coef_pad = jnp.pad(coeffs, ((0, 0), (1, 1), (1, 1)))

    def operate(field):
        return prec_scale * apply_k(apply_k(field, coef_pad), coef_pad) + obs_weight * field

    solution_field = jnp.zeros_like(right_side)
    residual = right_side
    direction = right_side
    norm_now = jnp.sum(residual * residual, axis=(0, 2))
    for iteration in range(ITERS):
        image = operate(direction)
        alpha = norm_now / jnp.sum(direction * image, axis=(0, 2))
        solution_field = solution_field + alpha[None, :, None] * direction
        residual = residual - alpha[None, :, None] * image
        norm_next = jnp.sum(residual * residual, axis=(0, 2))
        direction = residual + (norm_next / norm_now)[None, :, None] * direction
        norm_now = norm_next
    return solution_field, residual
```

```python
import jax
import jax.numpy as jnp
from jax import lax
from jax.experimental import pallas as pl
from jax.experimental.pallas import tpu as pltpu
from jax.sharding import PartitionSpec as P

PREC_SCALE = 0.01
RIM = 4
ROWS, COLS = 128, 256
REALS = 8
SLOTS = 1024
TILES, REGIONS = 16, 8
EXT = ROWS + 2 * RIM
WIDE = COLS + 128
CHUNKS = SLOTS // 128
DENSE = TILES * 128
GROUPS = 5
PIECE = EXT // 4
F32, BF16, I32 = jnp.float32, jnp.bfloat16, jnp.int32
VMEM_LIMIT = 48 * 1024 * 1024


def iota(shape, dim):
    return lax.broadcasted_iota(I32, shape, dim)


def contract_lanes(a, b):
    return lax.dot_general(a, b, (((1,), (1,)), ((), ())), preferred_element_type=F32)


def sort_body(count, cell_ref, value_ref, out):
    cell = cell_ref[...]
    index = iota((1, SLOTS), 1)
    live = index < count[0]
    key = (jnp.where(live, cell >> 8, 4096) * SLOTS + index).astype(F32)
    tall = jnp.transpose(jnp.broadcast_to(key, (128, SLOTS)))
    across = [jnp.broadcast_to(key[:, 128 * i : 128 * i + 128], (8, 128)) for i in range(CHUNKS)]
    below = [jnp.zeros((8, 128), F32) for _ in range(CHUNKS)]
    for j in range(SLOTS // 8):
        column = tall[8 * j : 8 * j + 8]
        for i in range(CHUNKS):
            below[i] = below[i] + jnp.where(column < across[i], 1.0, 0.0)
    rank = jnp.concatenate([jnp.sum(x, axis=0, keepdims=True) for x in below], axis=1).astype(I32)
    code = jnp.where(live, cell, 4096 * 256)
    value = value_ref[...]
    high = value.astype(BF16).astype(F32)
    rest = value - high
    middle = rest.astype(BF16).astype(F32)
    low = rest - middle
    left = jnp.concatenate(
        [
            high,
            middle,
            low,
            (code & 255).astype(F32),
            ((code >> 8) & 255).astype(F32),
            (code >> 16).astype(F32),
            jnp.zeros((5, SLOTS), F32),
        ],
        axis=0,
    ).astype(BF16)
    for k in range(SLOTS // 256):
        spot = jnp.where(iota((256, SLOTS), 0) + 256 * k == rank, 1.0, 0.0).astype(BF16)
        moved = contract_lanes(left, spot)
        values = (moved[0:8] + moved[8:16]) + moved[16:24]
        codes = moved[24:25] + 256.0 * moved[25:26] + 65536.0 * moved[26:27]
        for h in range(2):
            c = 2 * k + h
            out[8 * c : 8 * c + 8, :] = values[:, 128 * h : 128 * h + 128]
            out[64 + c : 65 + c, :] = codes[:, 128 * h : 128 * h + 128]


def scatter_body(recv, coef, south, north, b, w, cp, edge_l, edge_r, vals, code, ct, a, hits):
    first = lax.axis_index("tile") * ROWS - RIM
    low_cell = (first * COLS).astype(F32)
    high_cell = ((first + EXT) * COLS).astype(F32)
    cp[:, RIM : RIM + ROWS, :] = coef[...]
    cp[:, :RIM, :] = south[...]
    cp[:, RIM + ROWS :, :] = north[...]
    starts, lengths = [], []
    for s in range(TILES):
        cells = recv[s, 64:72, :]
        start = jnp.sum(jnp.where(cells < low_cell, 1.0, 0.0)).astype(I32)
        end = jnp.sum(jnp.where(cells < high_cell, 1.0, 0.0)).astype(I32)
        starts.append(start)
        lengths.append(end - start)
    most = lengths[0]
    for x in lengths[1:]:
        most = jnp.maximum(most, x)
    b[...] = jnp.zeros(b.shape, F32)
    hits[...] = jnp.zeros(hits.shape, F32)
    lane = iota((1, 128), 1)

    def one_round(k, carry):
        for s in range(TILES):
            here = jnp.minimum((starts[s] >> 7) + k, CHUNKS - 1)
            after = jnp.minimum(here + 1, CHUNKS - 1)
            shift = starts[s] & 127
            back = (128 - shift) & 127
            head = lane < 128 - shift
            inside = lane + 128 * k < lengths[s]
            v0 = pltpu.roll(recv[s, pl.ds(pl.multiple_of(here * 8, 8), 8), :], back, 1)
            v1 = pltpu.roll(recv[s, pl.ds(pl.multiple_of(after * 8, 8), 8), :], back, 1)
            c0 = pltpu.roll(jnp.broadcast_to(recv[s, pl.ds(64 + here, 1), :], (8, 128)), back, 1)
            c1 = pltpu.roll(jnp.broadcast_to(recv[s, pl.ds(64 + after, 1), :], (8, 128)), back, 1)
            value = jnp.where(inside, jnp.where(head, v0, v1), 0.0)
            local = jnp.where(head, c0, c1).astype(I32) - first * COLS
            vals[:, 128 * s : 128 * s + 128] = value
            code[:, 128 * s : 128 * s + 128] = jnp.where(inside, local, -COLS)
        row = code[...] >> 8
        column = code[0:1, :] & 255
        value = vals[...]
        high = value.astype(BF16).astype(F32)
        low = value - high
        ct[...] = jnp.where(iota((COLS, DENSE), 0) == column, 1.0, 0.0).astype(BF16)

        def piece(p, carry):
            base = p * PIECE
            for i in range(PIECE // 2):
                here = jnp.concatenate([row == base + 2 * i, row == base + 2 * i + 1], axis=0)
                both = jnp.concatenate([high, high], axis=0)
                a[16 * i : 16 * i + 16, :] = jnp.where(here, both, 0.0).astype(BF16)
                both = jnp.concatenate([low, low], axis=0)
                at = 8 * PIECE + 16 * i
                a[at : at + 16, :] = jnp.where(here, both, 0.0).astype(BF16)
            ones = jnp.where(iota((48, DENSE), 0) + base == row[0:1], 1.0, 0.0)
            a[16 * PIECE : 16 * PIECE + 48, :] = ones.astype(BF16)
            got = contract_lanes(a[...], ct[...])
            field = (got[: 8 * PIECE] + got[8 * PIECE : 16 * PIECE]) * 2.0
            b[pl.ds(base, PIECE)] += field.reshape(PIECE, REALS, COLS)
            hits[p] += got[16 * PIECE : 16 * PIECE + 40] * 2.0
            return carry

        return lax.fori_loop(0, EXT // PIECE, piece, carry)

    lax.fori_loop(0, (most + 127) >> 7, one_round, 0)

    for p in range(4):
        w[PIECE * p : PIECE * p + PIECE, :] = hits[p, 0:PIECE]
    lane8 = iota((8, 128), 1)
    for side, edge in ((0, edge_l), (1, edge_r)):
        cut = slice(0, 128) if side == 0 else slice(128, 256)
        for g in range(GROUPS):
            packed = jnp.zeros((8, 128), F32)
            packed_w = jnp.zeros((1, 128), F32)
            for j in range(min(32, EXT - 32 * g)):
                r = 32 * g + j
                turn = (4 * j + (0 if side == 0 else RIM)) % 128
                mine = (lane8 >= 4 * j) & (lane8 < 4 * j + 4)
                field, weight = b[r, :, cut], w[r : r + 1, cut]
                if turn:
                    field, weight = pltpu.roll(field, turn, 1), pltpu.roll(weight, turn, 1)
                packed = jnp.where(mine, field, packed)
                packed_w = jnp.where(mine[0:1], weight, packed_w)
            edge[8 * g : 8 * g + 8, :] = packed
            edge[40 + g : 41 + g, :] = packed_w
        edge[45:48, :] = jnp.zeros((3, 128), F32)
        keep = slice(0, RIM) if side == 0 else slice(128 - RIM, 128)
        for ch in range(4):
            turned = jnp.transpose(cp[ch, 0:128, cut])
            edge[48 + 4 * ch : 52 + 4 * ch, :] = turned[keep]
    tails = [cp[ch, 128:136, 128 * side : 128 * side + 128] for side in (0, 1) for ch in range(4)]
    turned = jnp.transpose(jnp.concatenate(tails + [jnp.zeros((64, 128), F32)], axis=0))
    edge_l[64:68, :] = turned[0:RIM]
    edge_r[64:68, :] = turned[128 - RIM : 128]
    edge_l[68:72, :] = jnp.zeros((4, 128), F32)
    edge_r[68:72, :] = jnp.zeros((4, 128), F32)


def krylov_body(b, w, cp, from_l, from_r, q_out, t_out, moments, own, b3, w3, c3, st, f, q3):
    region, tile = lax.axis_index("region"), lax.axis_index("tile")
    lane = iota((8, 128), 1)
    at_right, at_left = lane < RIM, lane >= 128 - RIM

    for ref in (b3, f, q3):
        ref[0] = jnp.zeros((REALS, WIDE), F32)
        ref[EXT + 1] = jnp.zeros((REALS, WIDE), F32)
    b3[1 : EXT + 1, :, 0:COLS] = b[...]
    w3[:, 0:COLS] = w[...]
    for r in range(EXT):
        g, j = r // 32, r % 32
        right, left = from_r[8 * g : 8 * g + 8, :], from_l[8 * g : 8 * g + 8, :]
        right_w, left_w = from_r[40 + g : 41 + g, :], from_l[40 + g : 41 + g, :]
        turn = (128 - 4 * j) % 128
        if turn:
            right, right_w = pltpu.roll(right, turn, 1), pltpu.roll(right_w, turn, 1)
        turn = (252 - 4 * j) % 128
        if turn:
            left, left_w = pltpu.roll(left, turn, 1), pltpu.roll(left_w, turn, 1)
        b3[r + 1, :, COLS:] = jnp.where(at_right, right, jnp.where(at_left, left, 0.0))
        w3[r : r + 1, COLS:] = jnp.where(
            at_right[0:1], right_w, jnp.where(at_left[0:1], left_w, 0.0)
        )
    c3[:, 0:8, :] = jnp.zeros((4, 8, WIDE), F32)
    c3[:, EXT + 8 :, :] = jnp.zeros((4, 8, WIDE), F32)
    c3[:, 8 : EXT + 8, 0:COLS] = cp[...]
    blank = jnp.zeros((128 - 2 * RIM, 128), F32)
    for ch in range(4):
        s = slice(48 + 4 * ch, 52 + 4 * ch)
        c3[ch, 8:136, COLS:] = jnp.transpose(jnp.concatenate([from_r[s], blank, from_l[s]], axis=0))
    turned = jnp.transpose(jnp.concatenate([from_r[64:68], blank, from_l[64:68]], axis=0))
    for ch in range(4):
        tail = jnp.where(at_right, turned[8 * ch : 8 * ch + 8], 0.0)
        tail = tail + jnp.where(at_left, turned[32 + 8 * ch : 40 + 8 * ch], 0.0)
        c3[ch, 136:144, COLS:] = tail

    largest = jnp.ones((8, WIDE), F32)
    for ch in range(4):
        for i in range(EXT // 8):
            largest = jnp.maximum(largest, jnp.abs(c3[ch, 8 + 8 * i : 16 + 8 * i, :]))
    scale = 1.0 / jnp.max(jnp.max(largest, axis=0, keepdims=True), axis=1, keepdims=True)
    w3[...] = w3[...] * (scale * scale)

    lane3 = iota((8, WIDE), 1)
    gx = jnp.where(lane3 >= WIDE - RIM, lane3 - WIDE, lane3) + region * COLS
    inside_x = (gx >= 0) & (gx < REGIONS * COLS) & ((lane3 < COLS + RIM) | (lane3 >= WIDE - RIM))

    def east(x):
        return pltpu.roll(x, WIDE - 1, 1)

    def west(x):
        return pltpu.roll(x, 1, 1)

    def coefficients(i, carry):
        at = 8 + 8 * i
        gy = tile * ROWS - RIM + 8 * i + iota((8, WIDE), 0)
        keep = jnp.where(inside_x & (gy >= 0) & (gy < TILES * ROWS), scale, 0.0)

        def near(ch, dy):
            if dy == 0:
                return c3[ch, pl.ds(pl.multiple_of(at, 8), 8), :]
            if dy == 1:
                ahead = c3[ch, pl.ds(pl.multiple_of(at + 8, 8), 8), :]
                return jnp.concatenate([near(ch, 0)[1:8], ahead[0:1]], axis=0)
            behind = c3[ch, pl.ds(pl.multiple_of(at - 8, 8), 8), :]
            return jnp.concatenate([behind[7:8], near(ch, 0)[0:7]], axis=0)

        h11, h22, kappa = near(0, 0), near(1, 0), near(3, 0)
        e = 0.5 * (east(h11) + h11)
        wst = 0.5 * (west(h11) + h11)
        n = 0.5 * (near(1, 1) + h22)
        s = 0.5 * (near(1, -1) + h22)
        m = near(2, 0)
        me, mw, mn, ms = east(m), west(m), near(2, 1), near(2, -1)
        rows = pl.ds(pl.multiple_of(8 * i, 8), 8)
        st[0, rows, :] = keep * (kappa + ((e + wst) + (n + s)))
        st[1, rows, :] = -keep * e
        st[2, rows, :] = -keep * wst
        st[3, rows, :] = -keep * n
        st[4, rows, :] = -keep * s
        quarter = 0.25 * keep
        st[5, rows, :] = -quarter * (me + mn)
        st[6, rows, :] = quarter * (mw + mn)
        st[7, rows, :] = quarter * (me + ms)
        st[8, rows, :] = -quarter * (mw + ms)
        return carry

    lax.fori_loop(0, EXT // 8, coefficients, 0)

    def three(ref, r):
        x = ref[r + 1]
        return x, east(x), west(x)

    def apply(src, start, count, put):
        def block(i, carry):
            below, here = carry
            for d in range(8):
                r = start + 8 * i + d
                above = three(src, r + 1)
                c = [st[k, pl.ds(r, 1), :] for k in range(9)]
                total = c[0] * here[0] + c[1] * here[1] + c[2] * here[2]
                total = total + (c[3] * above[0] + c[5] * above[1] + c[6] * above[2])
                total = total + (c[4] * below[0] + c[7] * below[1] + c[8] * below[2])
                put(r, total)
                below, here = here, above
            return below, here

        lax.fori_loop(0, count, block, (three(src, start - 1), three(src, start)))

    def put_f(r, total):
        f[r + 1] = total

    def put_q(r, total):
        value = PREC_SCALE * total + w3[pl.ds(r, 1), :] * b3[r + 1]
        q3[r + 1] = value

    def put_t(r, total):
        value = PREC_SCALE * total[:, :COLS] + w3[pl.ds(r, 1), 0:COLS] * q3[r + 1, :, 0:COLS]
        t_out[r - RIM] = value
        q_out[r - RIM] = q3[r + 1, :, 0:COLS]

    apply(b3, 0, EXT // 8, put_f)
    apply(f, 0, EXT // 8, put_q)
    apply(q3, 0, EXT // 8, put_f)
    apply(f, RIM, ROWS // 8, put_t)

    zero = jnp.zeros((REALS, COLS), F32)

    def first(i, acc):
        bb, bq, bt = acc
        for d in range(8):
            r = 8 * i + d
            x = b[r + RIM]
            bb, bq, bt = bb + x * x, bq + x * q_out[r], bt + x * t_out[r]
        return bb, bq, bt

    def total(x):
        return jnp.sum(x, axis=1, keepdims=True)

    bb, bq, bt = [total(x) for x in lax.fori_loop(0, ROWS // 8, first, (zero, zero, zero))]
    safe = jnp.where(bb > 0.0, bb, 1.0)
    sigma, tau = bq / safe, bt / safe

    def second(i, acc):
        uu, uz = acc
        for d in range(8):
            r = 8 * i + d
            x = b[r + RIM]
            u = q_out[r] - sigma * x
            uu, uz = uu + u * u, uz + u * (t_out[r] - tau * x)
        return uu, uz

    uu, uz = [total(x) for x in lax.fori_loop(0, ROWS // 8, second, (zero, zero))]
    mu = uz / jnp.where(uu > 0.0, uu, 1.0)
    inverse = 1.0 / (scale * scale)
    own[...] = jnp.broadcast_to(inverse, (8, 128))
    column = [jnp.broadcast_to(x, (8, 128)) for x in (bb, sigma, uu, tau, mu, inverse)]
    moments[...] = jnp.transpose(jnp.concatenate(column + [jnp.zeros((80, 128), F32)], axis=0))


def finish_body(moments, own, b, q, t, x_out, r_out):
    turned = jnp.transpose(moments[...])
    bb, sigma, uu, tau, mu, inverse = [turned[8 * m : 8 * m + 8] for m in range(6)]

    def total(x):
        return jnp.sum(x, axis=1, keepdims=True)

    norm0 = total(bb)
    alpha0 = norm0 / total(bb * sigma * inverse)
    a = alpha0 * inverse
    off = 1.0 - a * sigma
    norm1 = total(off * off * bb + a * a * uu)
    beta = norm1 / norm0
    grow = 1.0 + beta
    along = (grow - a * sigma) * (grow * sigma - a * tau) * bb
    curve = total(inverse * (along - a * (grow - a * mu) * uu))
    alpha1 = norm1 / curve
    mine = own[:, 0:1]
    a0 = alpha0 * mine
    a1 = alpha1 * mine

    def block(i, carry):
        for d in range(8):
            r = 8 * i + d
            x, y, z = b[r + RIM], q[r], t[r]
            r1 = x - a0 * y
            d1 = r1 + beta * x
            x_out[r] = alpha0 * x + alpha1 * d1
            r_out[r] = r1 - a1 * (grow * y - a0 * z)
        return carry

    lax.fori_loop(0, ROWS // 8, block, 0)


def call(body, shapes, scratch, *args, smem=0):
    vmem = pl.BlockSpec(memory_space=pltpu.VMEM)
    return pl.pallas_call(
        body,
        out_shape=[jax.ShapeDtypeStruct(s, F32) for s in shapes],
        in_specs=[pl.BlockSpec(memory_space=pltpu.SMEM)] * smem + [vmem] * (len(args) - smem),
        out_specs=[vmem] * len(shapes),
        scratch_shapes=scratch,
        compiler_params=pltpu.CompilerParams(vmem_limit_bytes=VMEM_LIMIT),
    )(*args)


def local(coeffs, obs_cell, obs_value, obs_count):
    up_tile = [(i, i + 1) for i in range(TILES - 1)]
    down_tile = [(j, i) for i, j in up_tile]
    up_region = [(i, i + 1) for i in range(REGIONS - 1)]
    down_region = [(j, i) for i, j in up_region]
    south = lax.ppermute(coeffs[:, ROWS - RIM :, :], "tile", up_tile)
    north = lax.ppermute(coeffs[:, :RIM, :], "tile", down_tile)
    (packed,) = call(
        sort_body, [(72, 128)], [], obs_count, obs_cell.reshape(1, SLOTS), obs_value, smem=1
    )
    recv = lax.all_to_all(jnp.broadcast_to(packed[None], (TILES, 72, 128)), "tile", 0, 0)
    b, w, cp, edge_l, edge_r = call(
        scatter_body,
        [(EXT, REALS, COLS), (EXT, COLS), (4, EXT, COLS), (72, 128), (72, 128)],
        [
            pltpu.VMEM((REALS, DENSE), F32),
            pltpu.VMEM((REALS, DENSE), I32),
            pltpu.VMEM((COLS, DENSE), BF16),
            pltpu.VMEM((16 * PIECE + 48, DENSE), BF16),
            pltpu.VMEM((4, 40, COLS), F32),
        ],
        recv,
        coeffs,
        south,
        north,
    )
    from_l = lax.ppermute(edge_r, "region", up_region)
    from_r = lax.ppermute(edge_l, "region", down_region)
    field = (ROWS, REALS, COLS)
    q, t, moments, own = call(
        krylov_body,
        [field, field, (128, 128), (8, 128)],
        [
            pltpu.VMEM((EXT + 2, REALS, WIDE), F32),
            pltpu.VMEM((EXT, WIDE), F32),
            pltpu.VMEM((4, EXT + 16, WIDE), F32),
            pltpu.VMEM((9, EXT, WIDE), F32),
            pltpu.VMEM((EXT + 2, REALS, WIDE), F32),
            pltpu.VMEM((EXT + 2, REALS, WIDE), F32),
        ],
        b,
        w,
        cp,
        from_l,
        from_r,
    )
    shared = lax.all_to_all(moments, ("region", "tile"), 0, 0, tiled=True)
    return tuple(call(finish_body, [field, field], [], shared, own, b, q, t))


def solution(mesh):
    placed = (
        P(None, "tile", "region"),
        P(("region", "tile")),
        P(None, ("region", "tile")),
        P(("region", "tile")),
    )
    return jax.shard_map(
        local,
        mesh=mesh,
        in_specs=placed,
        out_specs=(P("tile", None, "region"), P("tile", None, "region")),
        check_vma=False,
    )
```

```python
import jax
import jax.numpy as jnp
from jax import lax
from jax.experimental import pallas as pl
from jax.experimental.pallas import tpu as pltpu
from jax.sharding import PartitionSpec as P

PREC_SCALE = 0.01
RIM = 4
ROWS, COLS = 128, 256
REALS = 8
SLOTS = 1024
TILES, REGIONS = 16, 8
EXT = ROWS + 2 * RIM
WIDE = COLS + 128
CHUNKS = SLOTS // 128
SHARE = 96
DENSE = TILES * SHARE
GROUPS = 5
PART = 16
PIECE = EXT // 4
F32, BF16, I32 = jnp.float32, jnp.bfloat16, jnp.int32
VMEM_LIMIT = 48 * 1024 * 1024


def iota(shape, dim):
    return lax.broadcasted_iota(I32, shape, dim)


def contract_lanes(a, b):
    return lax.dot_general(a, b, (((1,), (1,)), ((), ())), preferred_element_type=F32)


def sort_body(count, cell_hbm, value_hbm, out, cell_ref, value_ref, arrive):
    copies = [
        pltpu.make_async_copy(cell_hbm, cell_ref, arrive.at[0]),
        pltpu.make_async_copy(value_hbm, value_ref, arrive.at[1]),
    ]
    for c in copies:
        c.start()
    copies[0].wait()
    cell = cell_ref[...]
    index = iota((1, SLOTS), 1)
    live = index < count[0]
    key = (jnp.where(live, cell >> 8, 4096) * SLOTS + index).astype(F32)
    tall = jnp.transpose(jnp.broadcast_to(key, (128, SLOTS)))
    across = [jnp.broadcast_to(key[:, 128 * i : 128 * i + 128], (8, 128)) for i in range(CHUNKS)]
    below = [jnp.zeros((8, 128), F32) for _ in range(CHUNKS)]
    for j in range(SLOTS // 8):
        column = tall[8 * j : 8 * j + 8]
        for i in range(CHUNKS):
            below[i] = below[i] + jnp.where(column < across[i], 1.0, 0.0)
    rank = jnp.concatenate([jnp.sum(x, axis=0, keepdims=True) for x in below], axis=1).astype(I32)
    code = jnp.where(live, cell, 4096 * 256)
    copies[1].wait()
    value = value_ref[...]
    high = value.astype(BF16).astype(F32)
    rest = value - high
    middle = rest.astype(BF16).astype(F32)
    low = rest - middle
    left = jnp.concatenate(
        [
            high,
            middle,
            low,
            (code & 255).astype(F32),
            ((code >> 8) & 255).astype(F32),
            (code >> 16).astype(F32),
            jnp.zeros((5, SLOTS), F32),
        ],
        axis=0,
    ).astype(BF16)
    for k in range(SLOTS // 256):
        spot = jnp.where(iota((256, SLOTS), 0) + 256 * k == rank, 1.0, 0.0).astype(BF16)
        moved = contract_lanes(left, spot)
        values = (moved[0:8] + moved[8:16]) + moved[16:24]
        codes = moved[24:25] + 256.0 * moved[25:26] + 65536.0 * moved[26:27]
        for h in range(2):
            c = 2 * k + h
            for s in range(TILES):
                out[s, 8 * c : 8 * c + 8, :] = values[:, 128 * h : 128 * h + 128]
                out[s, 64 + c : 65 + c, :] = codes[:, 128 * h : 128 * h + 128]


def scatter_body(recv, coef, south, north, b, w, cp, edge_l, edge_r, vals, code, ct, a, hits):
    first = lax.axis_index("tile") * ROWS - RIM
    low_cell = (first * COLS).astype(F32)
    high_cell = ((first + EXT) * COLS).astype(F32)
    cp[:, RIM : RIM + ROWS, :] = coef[...]
    tile = lax.axis_index("tile")
    cp[:, :RIM, :] = jnp.where(tile == 0, 0.0, south[...])
    cp[:, RIM + ROWS :, :] = jnp.where(tile == TILES - 1, 0.0, north[...])
    starts, lengths = [], []
    for s in range(TILES):
        cells = recv[s, 64:72, :]
        start = jnp.sum(jnp.where(cells < low_cell, 1.0, 0.0)).astype(I32)
        end = jnp.sum(jnp.where(cells < high_cell, 1.0, 0.0)).astype(I32)
        starts.append(start)
        lengths.append(end - start)
    most = lengths[0]
    for x in lengths[1:]:
        most = jnp.maximum(most, x)
    b[...] = jnp.zeros(b.shape, F32)
    hits[...] = jnp.zeros(hits.shape, F32)
    lane = iota((1, 128), 1)

    def one_round(k, carry):
        for chunk in range(DENSE // 128):
            value, local = jnp.zeros((REALS, 128), F32), jnp.full((8, 128), -COLS, I32)
            for s in range(128 * chunk // SHARE, (128 * chunk + 127) // SHARE + 1):
                begin = starts[s] + SHARE * k
                here = jnp.minimum(begin >> 7, CHUNKS - 1)
                after = jnp.minimum(here + 1, CHUNKS - 1)
                at = begin & 127
                offset = SHARE * s - 128 * chunk
                turn = (offset - at) & 127
                spot = lane - offset
                head = spot < 128 - at
                inside = (spot >= 0) & (spot < SHARE) & (spot + SHARE * k < lengths[s])
                v0 = pltpu.roll(recv[s, pl.ds(pl.multiple_of(here * 8, 8), 8), :], turn, 1)
                v1 = pltpu.roll(recv[s, pl.ds(pl.multiple_of(after * 8, 8), 8), :], turn, 1)
                c0 = jnp.broadcast_to(recv[s, pl.ds(64 + here, 1), :], (8, 128))
                c1 = jnp.broadcast_to(recv[s, pl.ds(64 + after, 1), :], (8, 128))
                c0, c1 = pltpu.roll(c0, turn, 1), pltpu.roll(c1, turn, 1)
                value = jnp.where(inside, jnp.where(head, v0, v1), value)
                cells = jnp.where(head, c0, c1).astype(I32) - first * COLS
                local = jnp.where(inside, cells, local)
            vals[:, 128 * chunk : 128 * chunk + 128] = value
            code[:, 128 * chunk : 128 * chunk + 128] = local
        row = code[...] >> 8
        column = code[0:1, :] & 255
        value = vals[...]
        high = value.astype(BF16).astype(F32)
        low = value - high
        ct[...] = jnp.where(iota((COLS, DENSE), 0) == column, 1.0, 0.0).astype(BF16)

        for p in range(4):
            base = p * PIECE
            for i in range(PIECE // 2):
                here = jnp.concatenate([row == base + 2 * i, row == base + 2 * i + 1], axis=0)
                both = jnp.concatenate([high, high], axis=0)
                a[p, 16 * i : 16 * i + 16, :] = jnp.where(here, both, 0.0).astype(BF16)
                both = jnp.concatenate([low, low], axis=0)
                at = 8 * PIECE + 16 * i
                a[p, at : at + 16, :] = jnp.where(here, both, 0.0).astype(BF16)
            ones = jnp.where(iota((48, DENSE), 0) + base == row[0:1], 1.0, 0.0)
            a[p, 16 * PIECE : 16 * PIECE + 48, :] = ones.astype(BF16)
            got = contract_lanes(a[p], ct[...])
            field = (got[: 8 * PIECE] + got[8 * PIECE : 16 * PIECE]) * 2.0
            b[base : base + PIECE] += field.reshape(PIECE, REALS, COLS)
            hits[p] += got[16 * PIECE : 16 * PIECE + 40] * 2.0
        return carry

    lax.fori_loop(0, (most + SHARE - 1) // SHARE, one_round, 0)

    for p in range(4):
        w[PIECE * p : PIECE * p + PIECE, :] = hits[p, 0:PIECE]
    lane8 = iota((8, 128), 1)
    for side, edge in ((0, edge_l), (1, edge_r)):
        cut = slice(0, 128) if side == 0 else slice(128, 256)
        for g in range(GROUPS):
            packed = jnp.zeros((8, 128), F32)
            packed_w = jnp.zeros((1, 128), F32)
            for j in range(min(32, EXT - 32 * g)):
                r = 32 * g + j
                turn = (4 * j + (0 if side == 0 else RIM)) % 128
                mine = (lane8 >= 4 * j) & (lane8 < 4 * j + 4)
                field, weight = b[r, :, cut], w[r : r + 1, cut]
                if turn:
                    field, weight = pltpu.roll(field, turn, 1), pltpu.roll(weight, turn, 1)
                packed = jnp.where(mine, field, packed)
                packed_w = jnp.where(mine[0:1], weight, packed_w)
            edge[8 * g : 8 * g + 8, :] = packed
            edge[40 + g : 41 + g, :] = packed_w
        edge[45:48, :] = jnp.zeros((3, 128), F32)
        keep = slice(0, RIM) if side == 0 else slice(128 - RIM, 128)
        for ch in range(4):
            turned = jnp.transpose(cp[ch, 0:128, cut])
            edge[48 + 4 * ch : 52 + 4 * ch, :] = turned[keep]
    tails = [cp[ch, 128:136, 128 * side : 128 * side + 128] for side in (0, 1) for ch in range(4)]
    turned = jnp.transpose(jnp.concatenate(tails + [jnp.zeros((64, 128), F32)], axis=0))
    edge_l[64:68, :] = turned[0:RIM]
    edge_r[64:68, :] = turned[128 - RIM : 128]
    edge_l[68:72, :] = jnp.zeros((4, 128), F32)
    edge_r[68:72, :] = jnp.zeros((4, 128), F32)


def krylov_body(b, w, cp, got_l, got_r, q_out, t_out, moments, own, b3, w3, c3, st, f, q3, from_l, from_r):
    region, tile = lax.axis_index("region"), lax.axis_index("tile")
    from_l[...] = jnp.where(region == 0, 0.0, got_l[...])
    from_r[...] = jnp.where(region == REGIONS - 1, 0.0, got_r[...])
    lane = iota((8, 128), 1)
    at_right, at_left = lane < RIM, lane >= 128 - RIM

    for ref in (b3, f, q3):
        ref[0] = jnp.zeros((REALS, WIDE), F32)
        ref[EXT + 1] = jnp.zeros((REALS, WIDE), F32)

    def east(x):
        return pltpu.roll(x, WIDE - 1, 1)

    def west(x):
        return pltpu.roll(x, 1, 1)

    w3[:, 0:COLS] = w[...]
    for r in range(EXT):
        g, j = r // 32, r % 32
        right, left = from_r[8 * g : 8 * g + 8, :], from_l[8 * g : 8 * g + 8, :]
        right_w, left_w = from_r[40 + g : 41 + g, :], from_l[40 + g : 41 + g, :]
        turn = (128 - 4 * j) % 128
        if turn:
            right, right_w = pltpu.roll(right, turn, 1), pltpu.roll(right_w, turn, 1)
        turn = (252 - 4 * j) % 128
        if turn:
            left, left_w = pltpu.roll(left, turn, 1), pltpu.roll(left_w, turn, 1)
        rim = jnp.where(at_right, right, jnp.where(at_left, left, 0.0))
        b3[r + 1, :, 0:COLS] = b[r]
        b3[r + 1, :, COLS:] = rim
        w3[r : r + 1, COLS:] = jnp.where(
            at_right[0:1], right_w, jnp.where(at_left[0:1], left_w, 0.0)
        )
    c3[:, 0:8, :] = jnp.zeros((4, 8, WIDE), F32)
    c3[:, EXT + 8 :, :] = jnp.zeros((4, 8, WIDE), F32)
    c3[:, 8 : EXT + 8, 0:COLS] = cp[...]
    blank = jnp.zeros((128 - 2 * RIM, 128), F32)
    for ch in range(4):
        s = slice(48 + 4 * ch, 52 + 4 * ch)
        c3[ch, 8:136, COLS:] = jnp.transpose(jnp.concatenate([from_r[s], blank, from_l[s]], axis=0))
    turned = jnp.transpose(jnp.concatenate([from_r[64:68], blank, from_l[64:68]], axis=0))
    for ch in range(4):
        tail = jnp.where(at_right, turned[8 * ch : 8 * ch + 8], 0.0)
        tail = tail + jnp.where(at_left, turned[32 + 8 * ch : 40 + 8 * ch], 0.0)
        c3[ch, 136:144, COLS:] = tail

    largest = jnp.ones((8, WIDE), F32)
    for ch in range(4):
        for i in range(EXT // 8):
            largest = jnp.maximum(largest, jnp.abs(c3[ch, 8 + 8 * i : 16 + 8 * i, :]))
    scale = 1.0 / jnp.max(jnp.max(largest, axis=0, keepdims=True), axis=1, keepdims=True)
    w3[...] = w3[...] * (scale * scale)

    lane3 = iota((8, WIDE), 1)
    gx = jnp.where(lane3 >= WIDE - RIM, lane3 - WIDE, lane3) + region * COLS
    here_x = (gx >= 0) & (gx < REGIONS * COLS) & ((lane3 < COLS + RIM) | (lane3 >= WIDE - RIM))
    east_x = here_x & (gx >= 0) & (gx + 1 < REGIONS * COLS) & (lane3 != COLS + RIM - 1)
    st[:, 0:1, :] = jnp.zeros((5, 1, WIDE), F32)
    st[:, EXT + 1 : EXT + 2, :] = jnp.zeros((5, 1, WIDE), F32)
    for i in range(EXT // 8):
        at = 8 + 8 * i
        gy = tile * ROWS - RIM + 8 * i + iota((8, WIDE), 0)
        here_y = (gy >= 0) & (gy < TILES * ROWS)
        north_y = (gy >= 0) & (gy + 1 < TILES * ROWS)
        south_y = (gy >= 1) & (gy < TILES * ROWS)

        def near(ch, dy):
            x = c3[ch, at : at + 8, :]
            if dy == 1:
                x = jnp.concatenate([x[1:8], c3[ch, at + 8 : at + 16, :][0:1]], axis=0)
            if dy == -1:
                x = jnp.concatenate([c3[ch, at - 8 : at, :][7:8], x[0:7]], axis=0)
            return x

        h11, h22, mixed = near(0, 0), near(1, 0), near(2, 0)
        e, wst = 0.5 * (east(h11) + h11), 0.5 * (west(h11) + h11)
        n, s = 0.5 * (near(1, 1) + h22), 0.5 * (near(1, -1) + h22)
        rows = slice(8 * i + 1, 8 * i + 9)
        side = east(mixed)
        st[0, rows, :] = jnp.where(here_x & here_y, scale * (near(3, 0) + ((e + wst) + (n + s))), 0.0)
        st[1, rows, :] = jnp.where(east_x & here_y, -scale * e, 0.0)
        st[2, rows, :] = jnp.where(here_x & north_y, -scale * n, 0.0)
        st[3, rows, :] = jnp.where(east_x & north_y, (-0.25 * scale) * (side + near(2, 1)), 0.0)
        st[4, rows, :] = jnp.where(east_x & south_y, (0.25 * scale) * (side + near(2, -1)), 0.0)

    def apply(src, start, count, finish, put):
        def cells(r):
            x = src[r + 1]
            return x, east(x), [st[k, r + 1 : r + 2, :] for k in range(5)]

        below, here = cells(start - 1), cells(start)
        for r in range(start, start + count):
            above = cells(r + 1)
            (v0, e0, c0), (v1, e1, c1), (v2, e2, c2) = below, here, above
            from_west = c1[1] * v1 + c0[3] * v0 + c2[4] * v2
            total = c1[0] * v1 + c1[1] * e1 + c1[2] * v2 + c0[2] * v0
            total = total + (c1[3] * e2 + c1[4] * e0) + west(from_west)
            put(r, finish(r, total))
            below, here = here, above

    def plain(r, total):
        return total

    def with_b(r, total):
        return PREC_SCALE * total + w3[pl.ds(r, 1), :] * b3[r + 1]

    sums = [jnp.zeros((REALS, COLS), F32) for _ in range(3)]

    def with_q(r, total):
        q = q3[r + 1, :, 0:COLS]
        x = b3[r + 1, :, 0:COLS]
        t = PREC_SCALE * total[:, :COLS] + w3[pl.ds(r, 1), 0:COLS] * q
        sums[:] = [sums[0] + x * x, sums[1] + x * q, sums[2] + x * t]
        return q, t

    def put_f(r, x):
        f[r + 1] = x

    def put_q(r, x):
        q3[r + 1] = x

    def put_t(r, x):
        q_out[r - RIM] = x[0]
        t_out[r - RIM] = x[1]

    apply(b3, 0, EXT, plain, put_f)
    apply(f, 0, EXT, with_b, put_q)
    apply(q3, 0, EXT, plain, put_f)
    apply(f, RIM, ROWS, with_q, put_t)

    def total(x):
        return jnp.sum(x, axis=1, keepdims=True)

    bb, bq, bt = [total(x) for x in sums]
    safe = jnp.where(bb > 0.0, bb, 1.0)
    sigma, tau = bq / safe, bt / safe

    def second(i, acc):
        uu, uz = acc
        for d in range(8):
            r = 8 * i + d
            x = b[r + RIM]
            u = q_out[r] - sigma * x
            uu, uz = uu + u * u, uz + u * (t_out[r] - tau * x)
        return uu, uz

    zero = jnp.zeros((REALS, COLS), F32)
    uu, uz = [total(x) for x in lax.fori_loop(0, ROWS // 8, second, (zero, zero))]
    mu = uz / jnp.where(uu > 0.0, uu, 1.0)
    inverse = 1.0 / (scale * scale)
    own[...] = jnp.broadcast_to(inverse, (8, 128))
    column = [jnp.broadcast_to(x, (8, 128)) for x in (bb, sigma, uu, tau, mu, inverse)]
    moments[...] = jnp.transpose(jnp.concatenate(column + [jnp.zeros((80, 128), F32)], axis=0))


def finish_body(moments, own, b, q, t, x_out, r_out, x_own, r_own, leave):
    turned = jnp.transpose(moments[...])
    bb, sigma, uu, tau, mu, inverse = [turned[8 * m : 8 * m + 8] for m in range(6)]

    def total(x):
        return jnp.sum(x, axis=1, keepdims=True)

    norm0 = total(bb)
    alpha0 = norm0 / total(bb * sigma * inverse)
    a = alpha0 * inverse
    off = 1.0 - a * sigma
    norm1 = total(off * off * bb + a * a * uu)
    beta = norm1 / norm0
    grow = 1.0 + beta
    along = (grow - a * sigma) * (grow * sigma - a * tau) * bb
    curve = total(inverse * (along - a * (grow - a * mu) * uu))
    alpha1 = norm1 / curve
    mine = own[:, 0:1]
    a0 = alpha0 * mine
    a1 = alpha1 * mine

    copies = []
    for i in range(ROWS // PART):
        for r in range(PART * i, PART * i + PART):
            x, y, z = b[r + RIM], q[r], t[r]
            r1 = x - a0 * y
            d1 = r1 + beta * x
            x_own[r] = alpha0 * x + alpha1 * d1
            r_own[r] = r1 - a1 * (grow * y - a0 * z)
        rows = pl.ds(PART * i, PART)
        copies.append(pltpu.make_async_copy(x_own.at[rows], x_out.at[rows], leave.at[0, i]))
        copies.append(pltpu.make_async_copy(r_own.at[rows], r_out.at[rows], leave.at[1, i]))
        for c in copies[-2:]:
            c.start()
    for c in copies:
        c.wait()


def call(body, shapes, scratch, *args, ins=None, outs=None, limit=VMEM_LIMIT):
    ins = ins or [pltpu.VMEM] * len(args)
    outs = outs or [pltpu.VMEM] * len(shapes)
    return pl.pallas_call(
        body,
        out_shape=[jax.ShapeDtypeStruct(s, F32) for s in shapes],
        in_specs=[pl.BlockSpec(memory_space=m) for m in ins],
        out_specs=[pl.BlockSpec(memory_space=m) for m in outs],
        scratch_shapes=scratch,
        compiler_params=pltpu.CompilerParams(vmem_limit_bytes=limit),
    )(*args)


def local(coeffs, obs_cell, obs_value, obs_count):
    def ring(x, axis, size, step):
        return lax.ppermute(x, axis, [(i, (i + step) % size) for i in range(size)])

    south = ring(coeffs[:, ROWS - RIM :, :], "tile", TILES, 1)
    north = ring(coeffs[:, :RIM, :], "tile", TILES, -1)
    (packed,) = call(
        sort_body,
        [(TILES, 72, 128)],
        [
            pltpu.VMEM((1, SLOTS), I32),
            pltpu.VMEM((REALS, SLOTS), F32),
            pltpu.SemaphoreType.DMA((2,)),
        ],
        obs_count,
        obs_cell.reshape(1, SLOTS),
        obs_value,
        ins=[pltpu.SMEM, pltpu.HBM, pltpu.HBM],
        limit=60 * 1024 * 1024,
    )
    packed, south, north = lax.optimization_barrier((packed, south, north))
    recv = lax.all_to_all(packed, "tile", 0, 0)
    b, w, cp, edge_l, edge_r = call(
        scatter_body,
        [(EXT, REALS, COLS), (EXT, COLS), (4, EXT, COLS), (72, 128), (72, 128)],
        [
            pltpu.VMEM((REALS, DENSE), F32),
            pltpu.VMEM((REALS, DENSE), I32),
            pltpu.VMEM((COLS, DENSE), BF16),
            pltpu.VMEM((4, 16 * PIECE + 48, DENSE), BF16),
            pltpu.VMEM((4, 40, COLS), F32),
        ],
        recv,
        coeffs,
        south,
        north,
    )
    from_l = ring(edge_r, "region", REGIONS, 1)
    from_r = ring(edge_l, "region", REGIONS, -1)
    field = (ROWS, REALS, COLS)
    q, t, moments, own = call(
        krylov_body,
        [field, field, (128, 128), (8, 128)],
        [
            pltpu.VMEM((EXT + 2, REALS, WIDE), F32),
            pltpu.VMEM((EXT, WIDE), F32),
            pltpu.VMEM((4, EXT + 16, WIDE), F32),
            pltpu.VMEM((5, EXT + 2, WIDE), F32),
            pltpu.VMEM((EXT + 2, REALS, WIDE), F32),
            pltpu.VMEM((EXT + 2, REALS, WIDE), F32),
            pltpu.VMEM((72, 128), F32),
            pltpu.VMEM((72, 128), F32),
        ],
        b,
        w,
        cp,
        from_l,
        from_r,
    )
    shared = lax.all_to_all(moments, ("region", "tile"), 0, 0, tiled=True)
    return tuple(
        call(
            finish_body,
            [field, field],
            [
                pltpu.VMEM(field, F32),
                pltpu.VMEM(field, F32),
                pltpu.SemaphoreType.DMA((2, ROWS // PART)),
            ],
            shared,
            own,
            b,
            q,
            t,
            outs=[pltpu.HBM, pltpu.HBM],
        )
    )


def solution(mesh):
    placed = (
        P(None, "tile", "region"),
        P(("region", "tile")),
        P(None, ("region", "tile")),
        P(("region", "tile")),
    )
    return jax.shard_map(
        local,
        mesh=mesh,
        in_specs=placed,
        out_specs=(P("tile", None, "region"), P("tile", None, "region")),
        check_vma=False,
    )
```

```python
import jax
import jax.numpy as jnp
from jax import lax
from jax.experimental import pallas as pl
from jax.experimental.pallas import tpu as pltpu
from jax.sharding import PartitionSpec as P

PREC_SCALE = 0.01
RIM = 4
ROWS, COLS = 128, 256
REALS = 8
SLOTS = 1024
TILES, REGIONS = 16, 8
EXT = ROWS + 2 * RIM
MESSAGE = 104
WIDE = COLS + 128
CHUNKS = SLOTS // 128
SHARE = 96
DENSE = TILES * SHARE
GROUPS = 5
PART = 16
PIECE = EXT // 4
F32, BF16, I32 = jnp.float32, jnp.bfloat16, jnp.int32
VMEM_LIMIT = 48 * 1024 * 1024


def iota(shape, dim):
    return lax.broadcasted_iota(I32, shape, dim)


def contract_lanes(a, b):
    return lax.dot_general(a, b, (((1,), (1,)), ((), ())), preferred_element_type=F32)


def sort_body(count, cell_hbm, value_hbm, coef_hbm, out, cell_ref, value_ref, low, high, arrive):
    copies = [
        pltpu.make_async_copy(cell_hbm, cell_ref, arrive.at[0]),
        pltpu.make_async_copy(value_hbm, value_ref, arrive.at[1]),
        pltpu.make_async_copy(coef_hbm.at[:, pl.ds(0, 8), :], low, arrive.at[2]),
        pltpu.make_async_copy(coef_hbm.at[:, pl.ds(ROWS - 8, 8), :], high, arrive.at[3]),
    ]
    for c in copies:
        c.start()
    copies[0].wait()
    cell = cell_ref[...]
    index = iota((1, SLOTS), 1)
    live = index < count[0]
    key = (jnp.where(live, cell >> 8, 4096) * SLOTS + index).astype(F32)
    tall = jnp.transpose(jnp.broadcast_to(key, (128, SLOTS)))
    across = [jnp.broadcast_to(key[:, 128 * i : 128 * i + 128], (8, 128)) for i in range(CHUNKS)]
    below = [jnp.zeros((8, 128), F32) for _ in range(CHUNKS)]
    for j in range(SLOTS // 8):
        column = tall[8 * j : 8 * j + 8]
        for i in range(CHUNKS):
            below[i] = below[i] + jnp.where(column < across[i], 1.0, 0.0)
    rank = jnp.concatenate([jnp.sum(x, axis=0, keepdims=True) for x in below], axis=1).astype(I32)
    code = jnp.where(live, cell, 4096 * 256)
    copies[1].wait()
    value = value_ref[...]
    top = value.astype(BF16).astype(F32)
    rest = value - top
    middle = rest.astype(BF16).astype(F32)
    left = jnp.concatenate(
        [
            top,
            middle,
            rest - middle,
            (code & 255).astype(F32),
            ((code >> 8) & 255).astype(F32),
            (code >> 16).astype(F32),
            jnp.zeros((5, SLOTS), F32),
        ],
        axis=0,
    ).astype(BF16)
    for k in range(SLOTS // 256):
        spot = jnp.where(iota((256, SLOTS), 0) + 256 * k == rank, 1.0, 0.0).astype(BF16)
        moved = contract_lanes(left, spot)
        values = (moved[0:8] + moved[8:16]) + moved[16:24]
        codes = moved[24:25] + 256.0 * moved[25:26] + 65536.0 * moved[26:27]
        for h in range(2):
            c = 2 * k + h
            for s in range(TILES):
                out[s, 8 * c : 8 * c + 8, :] = values[:, 128 * h : 128 * h + 128]
                out[s, 64 + c : 65 + c, :] = codes[:, 128 * h : 128 * h + 128]
    copies[2].wait()
    copies[3].wait()
    tile = lax.axis_index("tile")
    for ch in range(4):
        x, y = low[ch, 0:RIM, :], high[ch, 8 - RIM : 8, :]
        x = jnp.concatenate([x[:, 0:128], x[:, 128:256]], axis=0)
        y = jnp.concatenate([y[:, 0:128], y[:, 128:256]], axis=0)
        for s in range(TILES):
            out[s, 72 + 8 * ch : 80 + 8 * ch, :] = jnp.where(tile + 1 == s, y, x)


def scatter(recv, vals, code, one_round):
    first = lax.axis_index("tile") * ROWS - RIM
    low_cell = (first * COLS).astype(F32)
    high_cell = ((first + EXT) * COLS).astype(F32)
    starts, lengths = [], []
    for s in range(TILES):
        cells = recv[s, 64:72, :]
        start = jnp.sum(jnp.where(cells < low_cell, 1.0, 0.0)).astype(I32)
        end = jnp.sum(jnp.where(cells < high_cell, 1.0, 0.0)).astype(I32)
        starts.append(start)
        lengths.append(end - start)
    most = lengths[0]
    for x in lengths[1:]:
        most = jnp.maximum(most, x)
    lane = iota((1, 128), 1)

    def gather(k, carry):
        for chunk in range(DENSE // 128):
            value, local = jnp.zeros((REALS, 128), F32), jnp.full((8, 128), -COLS, I32)
            for s in range(128 * chunk // SHARE, (128 * chunk + 127) // SHARE + 1):
                begin = starts[s] + SHARE * k
                here = jnp.minimum(begin >> 7, CHUNKS - 1)
                after = jnp.minimum(here + 1, CHUNKS - 1)
                at = begin & 127
                offset = SHARE * s - 128 * chunk
                turn = (offset - at) & 127
                spot = lane - offset
                head = spot < 128 - at
                inside = (spot >= 0) & (spot < SHARE) & (spot + SHARE * k < lengths[s])
                v0 = pltpu.roll(recv[s, pl.ds(pl.multiple_of(here * 8, 8), 8), :], turn, 1)
                v1 = pltpu.roll(recv[s, pl.ds(pl.multiple_of(after * 8, 8), 8), :], turn, 1)
                c0 = jnp.broadcast_to(recv[s, pl.ds(64 + here, 1), :], (8, 128))
                c1 = jnp.broadcast_to(recv[s, pl.ds(64 + after, 1), :], (8, 128))
                c0, c1 = pltpu.roll(c0, turn, 1), pltpu.roll(c1, turn, 1)
                value = jnp.where(inside, jnp.where(head, v0, v1), value)
                cells = jnp.where(head, c0, c1).astype(I32) - first * COLS
                local = jnp.where(inside, cells, local)
            vals[:, 128 * chunk : 128 * chunk + 128] = value
            code[:, 128 * chunk : 128 * chunk + 128] = local
        value = vals[...]
        high = value.astype(BF16).astype(F32)
        one_round(code[...] >> 8, code[0:1, :] & 255, high, value - high)
        return carry

    lax.fori_loop(0, (most + SHARE - 1) // SHARE, gather, 0)


def edge_body(recv, coef, cp, edge_l, edge_r, vals, code, ct, a, packed):
    tile = lax.axis_index("tile")
    cp[:, RIM : RIM + ROWS, :] = coef[...]
    before, after = jnp.maximum(tile - 1, 0), jnp.minimum(tile + 1, TILES - 1)
    for ch in range(4):
        x = jnp.where(tile == 0, 0.0, recv[before, 72 + 8 * ch : 80 + 8 * ch, :])
        y = jnp.where(tile == TILES - 1, 0.0, recv[after, 72 + 8 * ch : 80 + 8 * ch, :])
        for h in range(2):
            cp[ch, 0:RIM, 128 * h : 128 * h + 128] = x[RIM * h : RIM * h + RIM]
            cp[ch, RIM + ROWS : EXT, 128 * h : 128 * h + 128] = y[RIM * h : RIM * h + RIM]
    packed[...] = jnp.zeros(packed.shape, F32)

    def one_round(row, column, high, low):
        near = row[0:1]
        spot = (near & 31) * 4 + column
        spot = jnp.where(column >= COLS - RIM, spot + (128 - COLS + RIM), spot)
        spot = jnp.where((column < RIM) | (column >= COLS - RIM), spot, -1)
        ct[...] = jnp.where(iota((COLS, DENSE), 0) == spot, 1.0, 0.0).astype(BF16)
        group = row >> 5
        for g in range(GROUPS):
            a[8 * g : 8 * g + 8, :] = jnp.where(group == g, high, 0.0).astype(BF16)
            a[40 + 8 * g : 48 + 8 * g, :] = jnp.where(group == g, low, 0.0).astype(BF16)
        ones = jnp.where(iota((16, DENSE), 0) == group[0:1], 1.0, 0.0)
        a[80:96, :] = ones.astype(BF16)
        got = contract_lanes(a[...], ct[...])
        packed[0:40, :] += (got[0:40] + got[40:80]) * 2.0
        packed[40:48, :] += got[80:88] * 2.0

    scatter(recv, vals, code, one_round)

    for side, edge in ((0, edge_l), (1, edge_r)):
        cut = slice(0, 128) if side == 0 else slice(128, 256)
        edge[0:48, :] = packed[:, cut]
        keep = slice(0, RIM) if side == 0 else slice(128 - RIM, 128)
        for ch in range(4):
            turned = jnp.transpose(cp[ch, 0:128, cut])
            edge[48 + 4 * ch : 52 + 4 * ch, :] = turned[keep]
    tails = [cp[ch, 128:136, 128 * side : 128 * side + 128] for side in (0, 1) for ch in range(4)]
    turned = jnp.transpose(jnp.concatenate(tails + [jnp.zeros((64, 128), F32)], axis=0))
    edge_l[64:68, :] = turned[0:RIM]
    edge_r[64:68, :] = turned[128 - RIM : 128]
    edge_l[68:72, :] = jnp.zeros((4, 128), F32)
    edge_r[68:72, :] = jnp.zeros((4, 128), F32)


def scatter_body(recv, b, w, vals, code, ct, a, hits):
    b[...] = jnp.zeros(b.shape, F32)
    hits[...] = jnp.zeros(hits.shape, F32)

    def one_round(row, column, high, low):
        ct[...] = jnp.where(iota((COLS, DENSE), 0) == column, 1.0, 0.0).astype(BF16)
        for p in range(4):
            base = p * PIECE
            for i in range(PIECE // 2):
                here = jnp.concatenate([row == base + 2 * i, row == base + 2 * i + 1], axis=0)
                both = jnp.concatenate([high, high], axis=0)
                a[p, 16 * i : 16 * i + 16, :] = jnp.where(here, both, 0.0).astype(BF16)
                both = jnp.concatenate([low, low], axis=0)
                at = 8 * PIECE + 16 * i
                a[p, at : at + 16, :] = jnp.where(here, both, 0.0).astype(BF16)
            ones = jnp.where(iota((48, DENSE), 0) + base == row[0:1], 1.0, 0.0)
            a[p, 16 * PIECE : 16 * PIECE + 48, :] = ones.astype(BF16)
            got = contract_lanes(a[p], ct[...])
            field = (got[: 8 * PIECE] + got[8 * PIECE : 16 * PIECE]) * 2.0
            b[base : base + PIECE] += field.reshape(PIECE, REALS, COLS)
            hits[p] += got[16 * PIECE : 16 * PIECE + 40] * 2.0

    scatter(recv, vals, code, one_round)
    for p in range(4):
        w[PIECE * p : PIECE * p + PIECE, :] = hits[p, 0:PIECE]


def krylov_body(b, w, cp, got_l, got_r, q_out, t_out, moments, own, b3, w3, c3, st, f, q3, from_l, from_r):
    region, tile = lax.axis_index("region"), lax.axis_index("tile")
    from_l[...] = jnp.where(region == 0, 0.0, got_l[...])
    from_r[...] = jnp.where(region == REGIONS - 1, 0.0, got_r[...])
    lane = iota((8, 128), 1)
    at_right, at_left = lane < RIM, lane >= 128 - RIM

    for ref in (b3, f, q3):
        ref[0] = jnp.zeros((REALS, WIDE), F32)
        ref[EXT + 1] = jnp.zeros((REALS, WIDE), F32)

    def east(x):
        return pltpu.roll(x, WIDE - 1, 1)

    def west(x):
        return pltpu.roll(x, 1, 1)

    w3[:, 0:COLS] = w[...]
    for r in range(EXT):
        g, j = r // 32, r % 32
        right, left = from_r[8 * g : 8 * g + 8, :], from_l[8 * g : 8 * g + 8, :]
        right_w, left_w = from_r[40 + g : 41 + g, :], from_l[40 + g : 41 + g, :]
        turn = (128 - 4 * j) % 128
        if turn:
            right, right_w = pltpu.roll(right, turn, 1), pltpu.roll(right_w, turn, 1)
        turn = (252 - 4 * j) % 128
        if turn:
            left, left_w = pltpu.roll(left, turn, 1), pltpu.roll(left_w, turn, 1)
        rim = jnp.where(at_right, right, jnp.where(at_left, left, 0.0))
        b3[r + 1, :, 0:COLS] = b[r]
        b3[r + 1, :, COLS:] = rim
        w3[r : r + 1, COLS:] = jnp.where(
            at_right[0:1], right_w, jnp.where(at_left[0:1], left_w, 0.0)
        )
    c3[:, 0:8, :] = jnp.zeros((4, 8, WIDE), F32)
    c3[:, EXT + 8 :, :] = jnp.zeros((4, 8, WIDE), F32)
    c3[:, 8 : EXT + 8, 0:COLS] = cp[...]
    blank = jnp.zeros((128 - 2 * RIM, 128), F32)
    for ch in range(4):
        s = slice(48 + 4 * ch, 52 + 4 * ch)
        c3[ch, 8:136, COLS:] = jnp.transpose(jnp.concatenate([from_r[s], blank, from_l[s]], axis=0))
    turned = jnp.transpose(jnp.concatenate([from_r[64:68], blank, from_l[64:68]], axis=0))
    for ch in range(4):
        tail = jnp.where(at_right, turned[8 * ch : 8 * ch + 8], 0.0)
        tail = tail + jnp.where(at_left, turned[32 + 8 * ch : 40 + 8 * ch], 0.0)
        c3[ch, 136:144, COLS:] = tail

    largest = jnp.ones((8, WIDE), F32)
    for ch in range(4):
        for i in range(EXT // 8):
            largest = jnp.maximum(largest, jnp.abs(c3[ch, 8 + 8 * i : 16 + 8 * i, :]))
    scale = 1.0 / jnp.max(jnp.max(largest, axis=0, keepdims=True), axis=1, keepdims=True)
    w3[...] = w3[...] * (scale * scale)

    lane3 = iota((8, WIDE), 1)
    gx = jnp.where(lane3 >= WIDE - RIM, lane3 - WIDE, lane3) + region * COLS
    here_x = (gx >= 0) & (gx < REGIONS * COLS) & ((lane3 < COLS + RIM) | (lane3 >= WIDE - RIM))
    east_x = here_x & (gx >= 0) & (gx + 1 < REGIONS * COLS) & (lane3 != COLS + RIM - 1)
    st[:, 0:1, :] = jnp.zeros((5, 1, WIDE), F32)
    st[:, EXT + 1 : EXT + 2, :] = jnp.zeros((5, 1, WIDE), F32)
    for i in range(EXT // 8):
        at = 8 + 8 * i
        gy = tile * ROWS - RIM + 8 * i + iota((8, WIDE), 0)
        here_y = (gy >= 0) & (gy < TILES * ROWS)
        north_y = (gy >= 0) & (gy + 1 < TILES * ROWS)
        south_y = (gy >= 1) & (gy < TILES * ROWS)

        def near(ch, dy):
            x = c3[ch, at : at + 8, :]
            if dy == 1:
                x = jnp.concatenate([x[1:8], c3[ch, at + 8 : at + 16, :][0:1]], axis=0)
            if dy == -1:
                x = jnp.concatenate([c3[ch, at - 8 : at, :][7:8], x[0:7]], axis=0)
            return x

        h11, h22, mixed = near(0, 0), near(1, 0), near(2, 0)
        e, wst = 0.5 * (east(h11) + h11), 0.5 * (west(h11) + h11)
        n, s = 0.5 * (near(1, 1) + h22), 0.5 * (near(1, -1) + h22)
        rows = slice(8 * i + 1, 8 * i + 9)
        side = east(mixed)
        st[0, rows, :] = jnp.where(here_x & here_y, scale * (near(3, 0) + ((e + wst) + (n + s))), 0.0)
        st[1, rows, :] = jnp.where(east_x & here_y, -scale * e, 0.0)
        st[2, rows, :] = jnp.where(here_x & north_y, -scale * n, 0.0)
        st[3, rows, :] = jnp.where(east_x & north_y, (-0.25 * scale) * (side + near(2, 1)), 0.0)
        st[4, rows, :] = jnp.where(east_x & south_y, (0.25 * scale) * (side + near(2, -1)), 0.0)

    def apply(src, start, count, finish, put):
        def cells(r):
            x = src[r + 1]
            return x, east(x), [st[k, r + 1 : r + 2, :] for k in range(5)]

        below, here = cells(start - 1), cells(start)
        for r in range(start, start + count):
            above = cells(r + 1)
            (v0, e0, c0), (v1, e1, c1), (v2, e2, c2) = below, here, above
            from_west = c1[1] * v1 + c0[3] * v0 + c2[4] * v2
            total = c1[0] * v1 + c1[1] * e1 + c1[2] * v2 + c0[2] * v0
            total = total + (c1[3] * e2 + c1[4] * e0) + west(from_west)
            put(r, finish(r, total))
            below, here = here, above

    def plain(r, total):
        return total

    def with_b(r, total):
        return PREC_SCALE * total + w3[pl.ds(r, 1), :] * b3[r + 1]

    sums = [jnp.zeros((REALS, COLS), F32) for _ in range(3)]

    def with_q(r, total):
        q = q3[r + 1, :, 0:COLS]
        x = b3[r + 1, :, 0:COLS]
        t = PREC_SCALE * total[:, :COLS] + w3[pl.ds(r, 1), 0:COLS] * q
        sums[:] = [sums[0] + x * x, sums[1] + x * q, sums[2] + x * t]
        return q, t

    def put_f(r, x):
        f[r + 1] = x

    def put_q(r, x):
        q3[r + 1] = x

    def put_t(r, x):
        q_out[r - RIM] = x[0]
        t_out[r - RIM] = x[1]

    apply(b3, 0, EXT, plain, put_f)
    apply(f, 0, EXT, with_b, put_q)
    apply(q3, 0, EXT, plain, put_f)
    apply(f, RIM, ROWS, with_q, put_t)

    def total(x):
        return jnp.sum(x, axis=1, keepdims=True)

    bb, bq, bt = [total(x) for x in sums]
    safe = jnp.where(bb > 0.0, bb, 1.0)
    sigma, tau = bq / safe, bt / safe

    def second(i, acc):
        uu, uz = acc
        for d in range(8):
            r = 8 * i + d
            x = b[r + RIM]
            u = q_out[r] - sigma * x
            uu, uz = uu + u * u, uz + u * (t_out[r] - tau * x)
        return uu, uz

    zero = jnp.zeros((REALS, COLS), F32)
    uu, uz = [total(x) for x in lax.fori_loop(0, ROWS // 8, second, (zero, zero))]
    mu = uz / jnp.where(uu > 0.0, uu, 1.0)
    inverse = 1.0 / (scale * scale)
    own[...] = jnp.broadcast_to(inverse, (8, 128))
    column = [jnp.broadcast_to(x, (8, 128)) for x in (bb, sigma, uu, tau, mu, inverse)]
    moments[...] = jnp.transpose(jnp.concatenate(column + [jnp.zeros((80, 128), F32)], axis=0))


def finish_body(moments, own, b, q, t, x_out, r_out, x_own, r_own, leave):
    turned = jnp.transpose(moments[...])
    bb, sigma, uu, tau, mu, inverse = [turned[8 * m : 8 * m + 8] for m in range(6)]

    def total(x):
        return jnp.sum(x, axis=1, keepdims=True)

    norm0 = total(bb)
    alpha0 = norm0 / total(bb * sigma * inverse)
    a = alpha0 * inverse
    off = 1.0 - a * sigma
    norm1 = total(off * off * bb + a * a * uu)
    beta = norm1 / norm0
    grow = 1.0 + beta
    along = (grow - a * sigma) * (grow * sigma - a * tau) * bb
    curve = total(inverse * (along - a * (grow - a * mu) * uu))
    alpha1 = norm1 / curve
    mine = own[:, 0:1]
    a0 = alpha0 * mine
    a1 = alpha1 * mine

    copies = []
    for i in range(ROWS // PART):
        for r in range(PART * i, PART * i + PART):
            x, y, z = b[r + RIM], q[r], t[r]
            r1 = x - a0 * y
            d1 = r1 + beta * x
            x_own[r] = alpha0 * x + alpha1 * d1
            r_own[r] = r1 - a1 * (grow * y - a0 * z)
        rows = pl.ds(PART * i, PART)
        copies.append(pltpu.make_async_copy(x_own.at[rows], x_out.at[rows], leave.at[0, i]))
        copies.append(pltpu.make_async_copy(r_own.at[rows], r_out.at[rows], leave.at[1, i]))
        for c in copies[-2:]:
            c.start()
    for c in copies:
        c.wait()


def call(body, shapes, scratch, *args, ins=None, outs=None, limit=VMEM_LIMIT, cost=None):
    ins = ins or [pltpu.VMEM] * len(args)
    outs = outs or [pltpu.VMEM] * len(shapes)
    return pl.pallas_call(
        body,
        out_shape=[jax.ShapeDtypeStruct(s, F32) for s in shapes],
        in_specs=[pl.BlockSpec(memory_space=m) for m in ins],
        out_specs=[pl.BlockSpec(memory_space=m) for m in outs],
        scratch_shapes=scratch,
        compiler_params=pltpu.CompilerParams(vmem_limit_bytes=limit),
        cost_estimate=cost,
    )(*args)


def local(coeffs, obs_cell, obs_value, obs_count):
    def ring(x, axis, size, step):
        return lax.ppermute(x, axis, [(i, (i + step) % size) for i in range(size)])

    (packed,) = call(
        sort_body,
        [(TILES, MESSAGE, 128)],
        [
            pltpu.VMEM((1, SLOTS), I32),
            pltpu.VMEM((REALS, SLOTS), F32),
            pltpu.VMEM((4, 8, COLS), F32),
            pltpu.VMEM((4, 8, COLS), F32),
            pltpu.SemaphoreType.DMA((4,)),
        ],
        obs_count,
        obs_cell.reshape(1, SLOTS),
        obs_value,
        coeffs,
        ins=[pltpu.SMEM, pltpu.HBM, pltpu.HBM, pltpu.HBM],
        limit=60 * 1024 * 1024,
    )
    recv = lax.all_to_all(packed, "tile", 0, 0)
    cp, edge_l, edge_r = call(
        edge_body,
        [(4, EXT, COLS), (72, 128), (72, 128)],
        [
            pltpu.VMEM((REALS, DENSE), F32),
            pltpu.VMEM((REALS, DENSE), I32),
            pltpu.VMEM((COLS, DENSE), BF16),
            pltpu.VMEM((96, DENSE), BF16),
            pltpu.VMEM((48, COLS), F32),
        ],
        recv,
        coeffs,
    )
    b, w = call(
        scatter_body,
        [(EXT, REALS, COLS), (EXT, COLS)],
        [
            pltpu.VMEM((REALS, DENSE), F32),
            pltpu.VMEM((REALS, DENSE), I32),
            pltpu.VMEM((COLS, DENSE), BF16),
            pltpu.VMEM((4, 16 * PIECE + 48, DENSE), BF16),
            pltpu.VMEM((4, 40, COLS), F32),
        ],
        recv,
        cost=pl.CostEstimate(flops=2 * 2368 * DENSE * COLS, bytes_accessed=1 << 23, transcendentals=0),
    )
    from_l = ring(edge_r, "region", REGIONS, 1)
    from_r = ring(edge_l, "region", REGIONS, -1)
    field = (ROWS, REALS, COLS)
    q, t, moments, own = call(
        krylov_body,
        [field, field, (128, 128), (8, 128)],
        [
            pltpu.VMEM((EXT + 2, REALS, WIDE), F32),
            pltpu.VMEM((EXT, WIDE), F32),
            pltpu.VMEM((4, EXT + 16, WIDE), F32),
            pltpu.VMEM((5, EXT + 2, WIDE), F32),
            pltpu.VMEM((EXT + 2, REALS, WIDE), F32),
            pltpu.VMEM((EXT + 2, REALS, WIDE), F32),
            pltpu.VMEM((72, 128), F32),
            pltpu.VMEM((72, 128), F32),
        ],
        b,
        w,
        cp,
        from_l,
        from_r,
    )
    shared = lax.all_to_all(moments, ("region", "tile"), 0, 0, tiled=True)
    return tuple(
        call(
            finish_body,
            [field, field],
            [
                pltpu.VMEM(field, F32),
                pltpu.VMEM(field, F32),
                pltpu.SemaphoreType.DMA((2, ROWS // PART)),
            ],
            shared,
            own,
            b,
            q,
            t,
            outs=[pltpu.HBM, pltpu.HBM],
        )
    )


def solution(mesh):
    placed = (
        P(None, "tile", "region"),
        P(("region", "tile")),
        P(None, ("region", "tile")),
        P(("region", "tile")),
    )
    return jax.shard_map(
        local,
        mesh=mesh,
        in_specs=placed,
        out_specs=(P("tile", None, "region"), P("tile", None, "region")),
        check_vma=False,
    )
```

```python
import jax
import jax.numpy as jnp
from jax import lax
from jax.experimental import pallas as pl
from jax.experimental.pallas import tpu as pltpu
from jax.sharding import PartitionSpec as P

PREC_SCALE = 0.01
RIM = 4
ROWS, COLS = 128, 256
REALS = 8
SLOTS = 1024
TILES, REGIONS = 16, 8
EXT = ROWS + 2 * RIM
MESSAGE = 48
LISTED = 72
DEAD = 4096 * 256
WIDE = COLS + 128
CHUNKS = SLOTS // 128
SHARE = 96
DENSE = TILES * SHARE
GROUPS = 5
PART = 16
PIECE = EXT // 4
F32, BF16, I32 = jnp.float32, jnp.bfloat16, jnp.int32
VMEM_LIMIT = 48 * 1024 * 1024


def iota(shape, dim):
    return lax.broadcasted_iota(I32, shape, dim)


def contract_lanes(a, b):
    return lax.dot_general(a, b, (((1,), (1,)), ((), ())), preferred_element_type=F32)


def sort_body(count, cell_hbm, value_hbm, coef_hbm, out, listed, cell_ref, value_ref, coef, arrive):
    copies = [
        pltpu.make_async_copy(cell_hbm, cell_ref, arrive.at[0]),
        pltpu.make_async_copy(value_hbm, value_ref, arrive.at[1]),
        pltpu.make_async_copy(coef_hbm, coef, arrive.at[2]),
    ]
    for c in copies:
        c.start()
    copies[0].wait()
    cell = cell_ref[...]
    index = iota((1, SLOTS), 1)
    live = index < count[0]
    key = (jnp.where(live, cell >> 8, 4096) * SLOTS + index).astype(F32)
    tall = jnp.transpose(jnp.broadcast_to(key, (128, SLOTS)))
    across = [jnp.broadcast_to(key[:, 128 * i : 128 * i + 128], (8, 128)) for i in range(CHUNKS)]
    below = [jnp.zeros((8, 128), F32) for _ in range(CHUNKS)]
    for j in range(SLOTS // 8):
        column = tall[8 * j : 8 * j + 8]
        for i in range(CHUNKS):
            below[i] = below[i] + jnp.where(column < across[i], 1.0, 0.0)
    rank = jnp.concatenate([jnp.sum(x, axis=0, keepdims=True) for x in below], axis=1).astype(I32)
    code = jnp.where(live, cell, DEAD)
    copies[1].wait()
    value = value_ref[...]
    top = value.astype(BF16).astype(F32)
    rest = value - top
    middle = rest.astype(BF16).astype(F32)
    left = jnp.concatenate(
        [
            top,
            middle,
            rest - middle,
            (code & 255).astype(F32),
            ((code >> 8) & 255).astype(F32),
            (code >> 16).astype(F32),
            jnp.zeros((5, SLOTS), F32),
        ],
        axis=0,
    ).astype(BF16)
    for k in range(SLOTS // 256):
        spot = jnp.where(iota((256, SLOTS), 0) + 256 * k == rank, 1.0, 0.0).astype(BF16)
        moved = contract_lanes(left, spot)
        values = (moved[0:8] + moved[8:16]) + moved[16:24]
        codes = moved[24:25] + 256.0 * moved[25:26] + 65536.0 * moved[26:27]
        for h in range(2):
            c = 2 * k + h
            listed[8 * c : 8 * c + 8, :] = values[:, 128 * h : 128 * h + 128]
            listed[64 + c : 65 + c, :] = codes[:, 128 * h : 128 * h + 128]
    cells = listed[64:72, :]
    lane = iota((1, 128), 1)
    starts, lengths = [], []
    for s in range(TILES):
        edge = [float((ROWS * s - RIM) * COLS), float((ROWS * s + ROWS + RIM) * COLS)]
        start, end = [jnp.sum(jnp.where(cells < x, 1.0, 0.0)).astype(I32) for x in edge]
        starts.append(start)
        lengths.append(end - start)
    most = lengths[0]
    for x in lengths[1:]:
        most = jnp.maximum(most, x)
    for s in range(TILES):
        here = jnp.minimum(starts[s] >> 7, CHUNKS - 1)
        after = jnp.minimum(here + 1, CHUNKS - 1)
        at = starts[s] & 127
        turn = (128 - at) & 127
        head = lane < 128 - at
        v0 = pltpu.roll(listed[pl.ds(pl.multiple_of(here * 8, 8), 8), :], turn, 1)
        v1 = pltpu.roll(listed[pl.ds(pl.multiple_of(after * 8, 8), 8), :], turn, 1)
        c0 = pltpu.roll(listed[pl.ds(64 + here, 1), :], turn, 1)
        c1 = pltpu.roll(listed[pl.ds(64 + after, 1), :], turn, 1)
        out[s, 0:8, :] = jnp.where(head, v0, v1)
        out[s, 8:9, :] = jnp.where(lane < lengths[s], jnp.where(head, c0, c1), float(DEAD))
        out[s, 9:10, :] = jnp.full((1, 128), most.astype(F32))
        out[s, 10:11, :] = jnp.full((1, 128), lengths[s].astype(F32))
        out[s, 11:16, :] = jnp.zeros((5, 128), F32)
    copies[2].wait()
    tile = lax.axis_index("tile")
    for ch in range(4):
        x, y = coef[ch, 0:RIM, :], coef[ch, ROWS - RIM : ROWS, :]
        x = jnp.concatenate([x[:, 0:128], x[:, 128:256]], axis=0)
        y = jnp.concatenate([y[:, 0:128], y[:, 128:256]], axis=0)
        own = [
            jnp.transpose(coef[ch, :, 0:128])[0:RIM],
            jnp.transpose(coef[ch, :, 128:256])[128 - RIM : 128],
        ]
        own = jnp.concatenate(own, axis=0)
        for s in range(TILES):
            rows = jnp.where(tile == s, own, jnp.where(tile + 1 == s, y, x))
            out[s, 16 + 8 * ch : 24 + 8 * ch, :] = rows


def scatter(recv, whole, vals, code, one_round):
    first = lax.axis_index("tile") * ROWS - RIM
    lane = iota((1, 128), 1)
    most = recv[0, 10:11, :]
    for s in range(1, TILES):
        most = jnp.maximum(most, recv[s, 10:11, :])
    most = jnp.max(most).astype(I32)

    def put(chunk, value, cells):
        vals[:, 128 * chunk : 128 * chunk + 128] = value
        code[:, 128 * chunk : 128 * chunk + 128] = cells.astype(I32) - first * COLS

    def blank():
        return jnp.zeros((REALS, 128), F32), jnp.full((8, 128), float(DEAD), F32)

    def head_of_block():
        for chunk in range(DENSE // 128):
            value, cells = blank()
            for s in range(128 * chunk // SHARE, (128 * chunk + 127) // SHARE + 1):
                offset = SHARE * s - 128 * chunk
                x, y = recv[s, 0:8, :], jnp.broadcast_to(recv[s, 8:9, :], (8, 128))
                if offset % 128:
                    x, y = pltpu.roll(x, offset % 128, 1), pltpu.roll(y, offset % 128, 1)
                inside = (lane >= offset) & (lane < offset + SHARE)
                value, cells = jnp.where(inside, x, value), jnp.where(inside, y, cells)
            put(chunk, value, cells)

    def tail_of_block():
        each = 128 - SHARE
        per = 128 // each
        for chunk in range(DENSE // 128):
            value, cells = blank()
            for s in range(per * chunk, min(per * chunk + per, TILES)):
                offset = each * (s % per)
                turn = (offset - SHARE) % 128
                x = pltpu.roll(recv[s, 0:8, :], turn, 1)
                y = pltpu.roll(jnp.broadcast_to(recv[s, 8:9, :], (8, 128)), turn, 1)
                inside = (lane >= offset) & (lane < offset + each)
                value, cells = jnp.where(inside, x, value), jnp.where(inside, y, cells)
            put(chunk, value, cells)

    def beyond_block(k):
        low_cell = (first * COLS).astype(F32)
        high_cell = ((first + EXT) * COLS).astype(F32)
        starts, lengths = [], []
        for s in range(TILES):
            cells = whole[s, 64:72, :]
            start = jnp.sum(jnp.where(cells < low_cell, 1.0, 0.0)).astype(I32)
            end = jnp.sum(jnp.where(cells < high_cell, 1.0, 0.0)).astype(I32)
            starts.append(start)
            lengths.append(end - start)
        done = 128 + SHARE * k
        for chunk in range(DENSE // 128):
            value, cells = blank()
            for s in range(128 * chunk // SHARE, (128 * chunk + 127) // SHARE + 1):
                begin = starts[s] + done
                here = jnp.minimum(begin >> 7, CHUNKS - 1)
                after = jnp.minimum(here + 1, CHUNKS - 1)
                at = begin & 127
                offset = SHARE * s - 128 * chunk
                turn = (offset - at) & 127
                spot = lane - offset
                head = spot < 128 - at
                inside = (spot >= 0) & (spot < SHARE) & (spot + done < lengths[s])
                v0 = pltpu.roll(whole[s, pl.ds(pl.multiple_of(here * 8, 8), 8), :], turn, 1)
                v1 = pltpu.roll(whole[s, pl.ds(pl.multiple_of(after * 8, 8), 8), :], turn, 1)
                c0 = jnp.broadcast_to(whole[s, pl.ds(64 + here, 1), :], (8, 128))
                c1 = jnp.broadcast_to(whole[s, pl.ds(64 + after, 1), :], (8, 128))
                c0, c1 = pltpu.roll(c0, turn, 1), pltpu.roll(c1, turn, 1)
                value = jnp.where(inside, jnp.where(head, v0, v1), value)
                cells = jnp.where(inside, jnp.where(head, c0, c1), cells)
            put(chunk, value, cells)

    def step(k, carry):
        pl.when(k == 0)(head_of_block)
        pl.when(k == 1)(tail_of_block)
        pl.when(k >= 2)(lambda: beyond_block(k - 2))
        value = vals[...]
        high = value.astype(BF16).astype(F32)
        one_round(code[...] >> 8, code[0:1, :] & 255, high, value - high)
        return carry

    extra = jnp.where(most > SHARE, 1, 0) + (jnp.maximum(most - 128, 0) + SHARE - 1) // SHARE
    lax.fori_loop(0, 1 + extra, step, 0)


def beside(recv, ch):
    tile = lax.axis_index("tile")
    before, after = jnp.maximum(tile - 1, 0), jnp.minimum(tile + 1, TILES - 1)
    x = jnp.where(tile == 0, 0.0, recv[before, 16 + 8 * ch : 24 + 8 * ch, :])
    y = jnp.where(tile == TILES - 1, 0.0, recv[after, 16 + 8 * ch : 24 + 8 * ch, :])
    return x, y


def edge_body(recv, whole, edge_l, edge_r, vals, code, ct, a, packed):
    packed[...] = jnp.zeros(packed.shape, F32)

    def one_round(row, column, high, low):
        near = row[0:1]
        spot = (near & 31) * 4 + column
        spot = jnp.where(column >= COLS - RIM, spot + (128 - COLS + RIM), spot)
        spot = jnp.where((column < RIM) | (column >= COLS - RIM), spot, -1)
        ct[...] = jnp.where(iota((COLS, DENSE), 0) == spot, 1.0, 0.0).astype(BF16)
        group = row >> 5
        for g in range(GROUPS):
            a[8 * g : 8 * g + 8, :] = jnp.where(group == g, high, 0.0).astype(BF16)
            a[40 + 8 * g : 48 + 8 * g, :] = jnp.where(group == g, low, 0.0).astype(BF16)
        ones = jnp.where(iota((16, DENSE), 0) == group[0:1], 1.0, 0.0)
        a[80:96, :] = ones.astype(BF16)
        got = contract_lanes(a[...], ct[...])
        packed[0:40, :] += (got[0:40] + got[40:80]) * 2.0
        packed[40:48, :] += got[80:88] * 2.0

    scatter(recv, whole, vals, code, one_round)

    for side, edge in ((0, edge_l), (1, edge_r)):
        cut = slice(0, 128) if side == 0 else slice(128, 256)
        edge[0:48, :] = packed[:, cut]
        for ch in range(4):
            own = recv[lax.axis_index("tile"), 16 + 8 * ch : 24 + 8 * ch, :]
            edge[48 + 4 * ch : 52 + 4 * ch, :] = own[RIM * side : RIM * side + RIM]
    tails = [x[RIM * h : RIM * h + RIM] for h in (0, 1) for ch in range(4) for x in beside(recv, ch)]
    turned = jnp.transpose(jnp.concatenate(tails + [jnp.zeros((64, 128), F32)], axis=0))
    edge_l[64:68, :] = turned[0:RIM]
    edge_r[64:68, :] = turned[128 - RIM : 128]
    edge_l[68:72, :] = jnp.zeros((4, 128), F32)
    edge_r[68:72, :] = jnp.zeros((4, 128), F32)


def scatter_body(recv, whole, b, w, vals, code, ct, a, hits):
    b[...] = jnp.zeros(b.shape, F32)
    hits[...] = jnp.zeros(hits.shape, F32)

    def one_round(row, column, high, low):
        ct[...] = jnp.where(iota((COLS, DENSE), 0) == column, 1.0, 0.0).astype(BF16)
        for p in range(4):
            base = p * PIECE
            for i in range(PIECE // 2):
                here = jnp.concatenate([row == base + 2 * i, row == base + 2 * i + 1], axis=0)
                both = jnp.concatenate([high, high], axis=0)
                a[p, 16 * i : 16 * i + 16, :] = jnp.where(here, both, 0.0).astype(BF16)
                both = jnp.concatenate([low, low], axis=0)
                at = 8 * PIECE + 16 * i
                a[p, at : at + 16, :] = jnp.where(here, both, 0.0).astype(BF16)
            ones = jnp.where(iota((48, DENSE), 0) + base == row[0:1], 1.0, 0.0)
            a[p, 16 * PIECE : 16 * PIECE + 48, :] = ones.astype(BF16)
            got = contract_lanes(a[p], ct[...])
            field = (got[: 8 * PIECE] + got[8 * PIECE : 16 * PIECE]) * 2.0
            b[base : base + PIECE] += field.reshape(PIECE, REALS, COLS)
            hits[p] += got[16 * PIECE : 16 * PIECE + 40] * 2.0

    scatter(recv, whole, vals, code, one_round)
    for p in range(4):
        w[PIECE * p : PIECE * p + PIECE, :] = hits[p, 0:PIECE]


def krylov_body(b, w, coef, recv, got_l, got_r, q_out, t_out, moments, own, b3, w3, c3, st, f, q3, from_l, from_r):
    region, tile = lax.axis_index("region"), lax.axis_index("tile")
    from_l[...] = jnp.where(region == 0, 0.0, got_l[...])
    from_r[...] = jnp.where(region == REGIONS - 1, 0.0, got_r[...])
    lane = iota((8, 128), 1)
    at_right, at_left = lane < RIM, lane >= 128 - RIM

    for ref in (b3, f, q3):
        ref[0] = jnp.zeros((REALS, WIDE), F32)
        ref[EXT + 1] = jnp.zeros((REALS, WIDE), F32)

    def east(x):
        return pltpu.roll(x, WIDE - 1, 1)

    def west(x):
        return pltpu.roll(x, 1, 1)

    w3[:, 0:COLS] = w[...]
    for r in range(EXT):
        g, j = r // 32, r % 32
        right, left = from_r[8 * g : 8 * g + 8, :], from_l[8 * g : 8 * g + 8, :]
        right_w, left_w = from_r[40 + g : 41 + g, :], from_l[40 + g : 41 + g, :]
        turn = (128 - 4 * j) % 128
        if turn:
            right, right_w = pltpu.roll(right, turn, 1), pltpu.roll(right_w, turn, 1)
        turn = (252 - 4 * j) % 128
        if turn:
            left, left_w = pltpu.roll(left, turn, 1), pltpu.roll(left_w, turn, 1)
        rim = jnp.where(at_right, right, jnp.where(at_left, left, 0.0))
        b3[r + 1, :, 0:COLS] = b[r]
        b3[r + 1, :, COLS:] = rim
        w3[r : r + 1, COLS:] = jnp.where(
            at_right[0:1], right_w, jnp.where(at_left[0:1], left_w, 0.0)
        )
    c3[:, 0:8, :] = jnp.zeros((4, 8, WIDE), F32)
    c3[:, EXT + 8 :, :] = jnp.zeros((4, 8, WIDE), F32)
    blank = jnp.zeros((128 - 2 * RIM, 128), F32)
    turned = jnp.transpose(jnp.concatenate([from_r[64:68], blank, from_l[64:68]], axis=0))
    own_rows = slice(8 + RIM, 8 + RIM + ROWS)
    for ch in range(4):
        c3[ch, own_rows, 0:COLS] = coef[ch]
        south, north = beside(recv, ch)
        for h in range(2):
            half, cut = slice(RIM * h, RIM * h + RIM), slice(128 * h, 128 * h + 128)
            c3[ch, 8 : 8 + RIM, cut] = south[half]
            c3[ch, 8 + RIM + ROWS : 8 + EXT, cut] = north[half]
        s = slice(48 + 4 * ch, 52 + 4 * ch)
        c3[ch, own_rows, COLS:] = jnp.transpose(jnp.concatenate([from_r[s], blank, from_l[s]], axis=0))
        tail = jnp.where(at_right, turned[8 * ch : 8 * ch + 8], 0.0)
        tail = tail + jnp.where(at_left, turned[32 + 8 * ch : 40 + 8 * ch], 0.0)
        c3[ch, 8 : 8 + RIM, COLS:] = tail[0:RIM]
        c3[ch, 8 + RIM + ROWS : 8 + EXT, COLS:] = tail[RIM : 2 * RIM]

    largest = jnp.ones((8, WIDE), F32)
    for ch in range(4):
        for i in range(EXT // 8):
            largest = jnp.maximum(largest, jnp.abs(c3[ch, 8 + 8 * i : 16 + 8 * i, :]))
    scale = 1.0 / jnp.max(jnp.max(largest, axis=0, keepdims=True), axis=1, keepdims=True)
    w3[...] = w3[...] * (scale * scale)

    lane3 = iota((8, WIDE), 1)
    gx = jnp.where(lane3 >= WIDE - RIM, lane3 - WIDE, lane3) + region * COLS
    here_x = (gx >= 0) & (gx < REGIONS * COLS) & ((lane3 < COLS + RIM) | (lane3 >= WIDE - RIM))
    east_x = here_x & (gx >= 0) & (gx + 1 < REGIONS * COLS) & (lane3 != COLS + RIM - 1)
    st[:, 0:1, :] = jnp.zeros((5, 1, WIDE), F32)
    st[:, EXT + 1 : EXT + 2, :] = jnp.zeros((5, 1, WIDE), F32)
    for i in range(EXT // 8):
        at = 8 + 8 * i
        gy = tile * ROWS - RIM + 8 * i + iota((8, WIDE), 0)
        here_y = (gy >= 0) & (gy < TILES * ROWS)
        north_y = (gy >= 0) & (gy + 1 < TILES * ROWS)
        south_y = (gy >= 1) & (gy < TILES * ROWS)

        def near(ch, dy):
            x = c3[ch, at : at + 8, :]
            if dy == 1:
                x = jnp.concatenate([x[1:8], c3[ch, at + 8 : at + 16, :][0:1]], axis=0)
            if dy == -1:
                x = jnp.concatenate([c3[ch, at - 8 : at, :][7:8], x[0:7]], axis=0)
            return x

        h11, h22, mixed = near(0, 0), near(1, 0), near(2, 0)
        e, wst = 0.5 * (east(h11) + h11), 0.5 * (west(h11) + h11)
        n, s = 0.5 * (near(1, 1) + h22), 0.5 * (near(1, -1) + h22)
        rows = slice(8 * i + 1, 8 * i + 9)
        side = east(mixed)
        st[0, rows, :] = jnp.where(here_x & here_y, scale * (near(3, 0) + ((e + wst) + (n + s))), 0.0)
        st[1, rows, :] = jnp.where(east_x & here_y, -scale * e, 0.0)
        st[2, rows, :] = jnp.where(here_x & north_y, -scale * n, 0.0)
        st[3, rows, :] = jnp.where(east_x & north_y, (-0.25 * scale) * (side + near(2, 1)), 0.0)
        st[4, rows, :] = jnp.where(east_x & south_y, (0.25 * scale) * (side + near(2, -1)), 0.0)

    def apply(src, start, count, finish, put):
        def cells(r):
            x = src[r + 1]
            return x, east(x), [st[k, r + 1 : r + 2, :] for k in range(5)]

        below, here = cells(start - 1), cells(start)
        for r in range(start, start + count):
            above = cells(r + 1)
            (v0, e0, c0), (v1, e1, c1), (v2, e2, c2) = below, here, above
            from_west = c1[1] * v1 + c0[3] * v0 + c2[4] * v2
            total = c1[0] * v1 + c1[1] * e1 + c1[2] * v2 + c0[2] * v0
            total = total + (c1[3] * e2 + c1[4] * e0) + west(from_west)
            put(r, finish(r, total))
            below, here = here, above

    def plain(r, total):
        return total

    def with_b(r, total):
        return PREC_SCALE * total + w3[pl.ds(r, 1), :] * b3[r + 1]

    sums = [jnp.zeros((REALS, COLS), F32) for _ in range(3)]

    def with_q(r, total):
        q = q3[r + 1, :, 0:COLS]
        x = b3[r + 1, :, 0:COLS]
        t = PREC_SCALE * total[:, :COLS] + w3[pl.ds(r, 1), 0:COLS] * q
        sums[:] = [sums[0] + x * x, sums[1] + x * q, sums[2] + x * t]
        return q, t

    def put_f(r, x):
        f[r + 1] = x

    def put_q(r, x):
        q3[r + 1] = x

    def put_t(r, x):
        q_out[r - RIM] = x[0]
        t_out[r - RIM] = x[1]

    apply(b3, 0, EXT, plain, put_f)
    apply(f, 0, EXT, with_b, put_q)
    apply(q3, 0, EXT, plain, put_f)
    apply(f, RIM, ROWS, with_q, put_t)

    def total(x):
        return jnp.sum(x, axis=1, keepdims=True)

    bb, bq, bt = [total(x) for x in sums]
    safe = jnp.where(bb > 0.0, bb, 1.0)
    sigma, tau = bq / safe, bt / safe

    def second(i, acc):
        uu, uz = acc
        for d in range(8):
            r = 8 * i + d
            x = b[r + RIM]
            u = q_out[r] - sigma * x
            uu, uz = uu + u * u, uz + u * (t_out[r] - tau * x)
        return uu, uz

    zero = jnp.zeros((REALS, COLS), F32)
    uu, uz = [total(x) for x in lax.fori_loop(0, ROWS // 8, second, (zero, zero))]
    mu = uz / jnp.where(uu > 0.0, uu, 1.0)
    inverse = 1.0 / (scale * scale)
    own[...] = jnp.broadcast_to(inverse, (8, 128))
    column = [jnp.broadcast_to(x, (8, 128)) for x in (bb, sigma, uu, tau, mu, inverse)]
    moments[...] = jnp.transpose(jnp.concatenate(column + [jnp.zeros((80, 128), F32)], axis=0))


def finish_body(moments, own, b, q, t, x_out, r_out, x_own, r_own, leave):
    turned = jnp.transpose(moments[...])
    bb, sigma, uu, tau, mu, inverse = [turned[8 * m : 8 * m + 8] for m in range(6)]

    def total(x):
        return jnp.sum(x, axis=1, keepdims=True)

    norm0 = total(bb)
    alpha0 = norm0 / total(bb * sigma * inverse)
    a = alpha0 * inverse
    off = 1.0 - a * sigma
    norm1 = total(off * off * bb + a * a * uu)
    beta = norm1 / norm0
    grow = 1.0 + beta
    along = (grow - a * sigma) * (grow * sigma - a * tau) * bb
    curve = total(inverse * (along - a * (grow - a * mu) * uu))
    alpha1 = norm1 / curve
    mine = own[:, 0:1]
    a0 = alpha0 * mine
    a1 = alpha1 * mine

    copies = []
    for i in range(ROWS // PART):
        for r in range(PART * i, PART * i + PART):
            x, y, z = b[r + RIM], q[r], t[r]
            r1 = x - a0 * y
            d1 = r1 + beta * x
            x_own[r] = alpha0 * x + alpha1 * d1
            r_own[r] = r1 - a1 * (grow * y - a0 * z)
        rows = pl.ds(PART * i, PART)
        copies.append(pltpu.make_async_copy(x_own.at[rows], x_out.at[rows], leave.at[0, i]))
        copies.append(pltpu.make_async_copy(r_own.at[rows], r_out.at[rows], leave.at[1, i]))
        for c in copies[-2:]:
            c.start()
    for c in copies:
        c.wait()


def call(body, shapes, scratch, *args, ins=None, outs=None, limit=VMEM_LIMIT, cost=None):
    ins = ins or [pltpu.VMEM] * len(args)
    outs = outs or [pltpu.VMEM] * len(shapes)
    return pl.pallas_call(
        body,
        out_shape=[jax.ShapeDtypeStruct(s, F32) for s in shapes],
        in_specs=[pl.BlockSpec(memory_space=m) for m in ins],
        out_specs=[pl.BlockSpec(memory_space=m) for m in outs],
        scratch_shapes=scratch,
        compiler_params=pltpu.CompilerParams(vmem_limit_bytes=limit),
        cost_estimate=cost,
    )(*args)


def local(coeffs, obs_cell, obs_value, obs_count):
    def ring(x, axis, size, step):
        return lax.ppermute(x, axis, [(i, (i + step) % size) for i in range(size)])

    packed, listed = call(
        sort_body,
        [(TILES, MESSAGE, 128), (LISTED, 128)],
        [
            pltpu.VMEM((1, SLOTS), I32),
            pltpu.VMEM((REALS, SLOTS), F32),
            pltpu.VMEM((4, ROWS, COLS), F32),
            pltpu.SemaphoreType.DMA((3,)),
        ],
        obs_count,
        obs_cell.reshape(1, SLOTS),
        obs_value,
        coeffs,
        ins=[pltpu.SMEM, pltpu.HBM, pltpu.HBM, pltpu.HBM],
        limit=60 * 1024 * 1024,
    )
    recv = lax.all_to_all(packed, "tile", 0, 0)

    def share(x):
        return lax.all_to_all(jnp.broadcast_to(x[None], (TILES, LISTED, 128)), "tile", 0, 0)

    def skip(x):
        return jnp.zeros((TILES, LISTED, 128), F32)

    whole = lax.cond(jnp.max(recv[:, 9, 0]) > 128.0, share, skip, listed)
    edge_l, edge_r = call(
        edge_body,
        [(72, 128), (72, 128)],
        [
            pltpu.VMEM((REALS, DENSE), F32),
            pltpu.VMEM((REALS, DENSE), I32),
            pltpu.VMEM((COLS, DENSE), BF16),
            pltpu.VMEM((96, DENSE), BF16),
            pltpu.VMEM((48, COLS), F32),
        ],
        recv,
        whole,
    )
    b, w = call(
        scatter_body,
        [(EXT, REALS, COLS), (EXT, COLS)],
        [
            pltpu.VMEM((REALS, DENSE), F32),
            pltpu.VMEM((REALS, DENSE), I32),
            pltpu.VMEM((COLS, DENSE), BF16),
            pltpu.VMEM((4, 16 * PIECE + 48, DENSE), BF16),
            pltpu.VMEM((4, 40, COLS), F32),
        ],
        recv,
        whole,
        cost=pl.CostEstimate(flops=2 * 2368 * DENSE * COLS, bytes_accessed=1 << 23, transcendentals=0),
    )
    from_l = ring(edge_r, "region", REGIONS, 1)
    from_r = ring(edge_l, "region", REGIONS, -1)
    field = (ROWS, REALS, COLS)
    q, t, moments, own = call(
        krylov_body,
        [field, field, (128, 128), (8, 128)],
        [
            pltpu.VMEM((EXT + 2, REALS, WIDE), F32),
            pltpu.VMEM((EXT, WIDE), F32),
            pltpu.VMEM((4, EXT + 16, WIDE), F32),
            pltpu.VMEM((5, EXT + 2, WIDE), F32),
            pltpu.VMEM((EXT + 2, REALS, WIDE), F32),
            pltpu.VMEM((EXT + 2, REALS, WIDE), F32),
            pltpu.VMEM((72, 128), F32),
            pltpu.VMEM((72, 128), F32),
        ],
        b,
        w,
        coeffs,
        recv,
        from_l,
        from_r,
    )
    shared = lax.all_to_all(moments, ("region", "tile"), 0, 0, tiled=True)
    return tuple(
        call(
            finish_body,
            [field, field],
            [
                pltpu.VMEM(field, F32),
                pltpu.VMEM(field, F32),
                pltpu.SemaphoreType.DMA((2, ROWS // PART)),
            ],
            shared,
            own,
            b,
            q,
            t,
            outs=[pltpu.HBM, pltpu.HBM],
        )
    )


def solution(mesh):
    placed = (
        P(None, "tile", "region"),
        P(("region", "tile")),
        P(None, ("region", "tile")),
        P(("region", "tile")),
    )
    return jax.shard_map(
        local,
        mesh=mesh,
        in_specs=placed,
        out_specs=(P("tile", None, "region"), P("tile", None, "region")),
        check_vma=False,
    )
```

```python
import jax
import jax.numpy as jnp
from jax import lax
from jax.experimental import pallas as pl
from jax.experimental.pallas import tpu as pltpu
from jax.sharding import PartitionSpec as P

PREC_SCALE = 0.01
RIM = 4
ROWS, COLS = 128, 256
REALS = 8
SLOTS = 1024
TILES, REGIONS = 16, 8
EXT = ROWS + 2 * RIM
MESSAGE = 40
LISTED = 72
PLACE = (32, 16, 24, 10)
KEPT = (3, 4, 4, 3)
DEAD = 4096 * 256
WIDE = COLS + 128
CHUNKS = SLOTS // 128
SHARE = 96
DENSE = TILES * SHARE
GROUPS = 5
PART = 16
PIECE = EXT // 4
F32, BF16, I32 = jnp.float32, jnp.bfloat16, jnp.int32
VMEM_LIMIT = 48 * 1024 * 1024


def iota(shape, dim):
    return lax.broadcasted_iota(I32, shape, dim)


def contract_lanes(a, b):
    return lax.dot_general(a, b, (((1,), (1,)), ((), ())), preferred_element_type=F32)


def sort_body(count, cell_hbm, value_hbm, coef_hbm, out, listed, space, cell_ref, value_ref, coef, arrive):
    copies = [
        pltpu.make_async_copy(cell_hbm, cell_ref, arrive.at[0]),
        pltpu.make_async_copy(value_hbm, value_ref, arrive.at[1]),
        pltpu.make_async_copy(coef_hbm, coef, arrive.at[2]),
    ]
    for c in copies:
        c.start()
    copies[0].wait()
    cell = cell_ref[...]
    index = iota((1, SLOTS), 1)
    live = index < count[0]
    key = (jnp.where(live, cell >> 8, 4096) * SLOTS + index).astype(F32)
    tall = jnp.transpose(jnp.broadcast_to(key, (128, SLOTS)))
    across = [jnp.broadcast_to(key[:, 128 * i : 128 * i + 128], (8, 128)) for i in range(CHUNKS)]
    below = [jnp.zeros((8, 128), F32) for _ in range(CHUNKS)]
    for j in range(SLOTS // 8):
        column = tall[8 * j : 8 * j + 8]
        for i in range(CHUNKS):
            below[i] = below[i] + jnp.where(column < across[i], 1.0, 0.0)
    rank = jnp.concatenate([jnp.sum(x, axis=0, keepdims=True) for x in below], axis=1).astype(I32)
    code = jnp.where(live, cell, DEAD)
    copies[1].wait()
    value = value_ref[...]
    top = value.astype(BF16).astype(F32)
    rest = value - top
    middle = rest.astype(BF16).astype(F32)
    left = jnp.concatenate(
        [
            top,
            middle,
            rest - middle,
            (code & 255).astype(F32),
            ((code >> 8) & 255).astype(F32),
            (code >> 16).astype(F32),
            jnp.zeros((5, SLOTS), F32),
        ],
        axis=0,
    ).astype(BF16)
    for k in range(SLOTS // 256):
        spot = jnp.where(iota((256, SLOTS), 0) + 256 * k == rank, 1.0, 0.0).astype(BF16)
        moved = contract_lanes(left, spot)
        values = (moved[0:8] + moved[8:16]) + moved[16:24]
        codes = moved[24:25] + 256.0 * moved[25:26] + 65536.0 * moved[26:27]
        for h in range(2):
            c = 2 * k + h
            listed[8 * c : 8 * c + 8, :] = values[:, 128 * h : 128 * h + 128]
            listed[64 + c : 65 + c, :] = codes[:, 128 * h : 128 * h + 128]
    cells = listed[64:72, :]
    lane = iota((1, 128), 1)
    starts, lengths = [], []
    for s in range(TILES):
        edge = [float((ROWS * s - RIM) * COLS), float((ROWS * s + ROWS + RIM) * COLS)]
        start, end = [jnp.sum(jnp.where(cells < x, 1.0, 0.0)).astype(I32) for x in edge]
        starts.append(start)
        lengths.append(end - start)
    most = lengths[0]
    for x in lengths[1:]:
        most = jnp.maximum(most, x)
    for s in range(TILES):
        here = jnp.minimum(starts[s] >> 7, CHUNKS - 1)
        after = jnp.minimum(here + 1, CHUNKS - 1)
        at = starts[s] & 127
        turn = (128 - at) & 127
        head = lane < 128 - at
        v0 = pltpu.roll(listed[pl.ds(pl.multiple_of(here * 8, 8), 8), :], turn, 1)
        v1 = pltpu.roll(listed[pl.ds(pl.multiple_of(after * 8, 8), 8), :], turn, 1)
        c0 = pltpu.roll(listed[pl.ds(64 + here, 1), :], turn, 1)
        c1 = pltpu.roll(listed[pl.ds(64 + after, 1), :], turn, 1)
        out[s, 0:8, :] = jnp.where(head, v0, v1)
        out[s, 8:9, :] = jnp.where(lane < lengths[s], jnp.where(head, c0, c1), float(DEAD))
        counts = jnp.where(lane < 64, most.astype(F32), lengths[s].astype(F32))
        out[s, 9:10, :] = counts
        out[s, 38:40, :] = jnp.zeros((2, 128), F32)
    copies[2].wait()
    tile = lax.axis_index("tile")
    for ch in range(4):
        n = KEPT[ch]
        x, y = coef[ch, 0:n, :], coef[ch, ROWS - n : ROWS, :]
        x = jnp.concatenate([x[:, 0:128], x[:, 128:256]], axis=0)
        y = jnp.concatenate([y[:, 0:128], y[:, 128:256]], axis=0)
        for s in range(TILES):
            out[s, PLACE[ch] : PLACE[ch] + 2 * n, :] = jnp.where(tile + 1 == s, y, x)
        at = LISTED + 8 * ch
        listed[at : at + RIM, :] = jnp.transpose(coef[ch, :, 0:128])[0:RIM]
        listed[at + RIM : at + 8, :] = jnp.transpose(coef[ch, :, 128:256])[128 - RIM : 128]


def scatter(recv, whole, vals, code, one_round, block=True, beyond=True, fetch=None):
    first = lax.axis_index("tile") * ROWS - RIM
    lane = iota((1, 128), 1)
    most = recv[0, 9:10, :]
    for s in range(1, TILES):
        most = jnp.maximum(most, recv[s, 9:10, :])
    most = jnp.max(jnp.where(lane < 64, 0.0, most)).astype(I32)

    def put(chunk, value, cells):
        vals[:, 128 * chunk : 128 * chunk + 128] = value
        code[:, 128 * chunk : 128 * chunk + 128] = cells.astype(I32) - first * COLS

    def blank():
        return jnp.zeros((REALS, 128), F32), jnp.full((8, 128), float(DEAD), F32)

    def head_of_block():
        for chunk in range(DENSE // 128):
            value, cells = blank()
            for s in range(128 * chunk // SHARE, (128 * chunk + 127) // SHARE + 1):
                offset = SHARE * s - 128 * chunk
                x, y = recv[s, 0:8, :], jnp.broadcast_to(recv[s, 8:9, :], (8, 128))
                if offset % 128:
                    x, y = pltpu.roll(x, offset % 128, 1), pltpu.roll(y, offset % 128, 1)
                inside = (lane >= offset) & (lane < offset + SHARE)
                value, cells = jnp.where(inside, x, value), jnp.where(inside, y, cells)
            put(chunk, value, cells)

    def tail_of_block():
        each = 128 - SHARE
        per = 128 // each
        for chunk in range(DENSE // 128):
            value, cells = blank()
            for s in range(per * chunk, min(per * chunk + per, TILES)):
                offset = each * (s % per)
                turn = (offset - SHARE) % 128
                x = pltpu.roll(recv[s, 0:8, :], turn, 1)
                y = pltpu.roll(jnp.broadcast_to(recv[s, 8:9, :], (8, 128)), turn, 1)
                inside = (lane >= offset) & (lane < offset + each)
                value, cells = jnp.where(inside, x, value), jnp.where(inside, y, cells)
            put(chunk, value, cells)

    def beyond_block(k):
        low_cell = (first * COLS).astype(F32)
        high_cell = ((first + EXT) * COLS).astype(F32)
        starts, lengths = [], []
        for s in range(TILES):
            cells = whole[s, 64:72, :]
            start = jnp.sum(jnp.where(cells < low_cell, 1.0, 0.0)).astype(I32)
            end = jnp.sum(jnp.where(cells < high_cell, 1.0, 0.0)).astype(I32)
            starts.append(start)
            lengths.append(end - start)
        done = 128 + SHARE * k
        for chunk in range(DENSE // 128):
            value, cells = blank()
            for s in range(128 * chunk // SHARE, (128 * chunk + 127) // SHARE + 1):
                begin = starts[s] + done
                here = jnp.minimum(begin >> 7, CHUNKS - 1)
                after = jnp.minimum(here + 1, CHUNKS - 1)
                at = begin & 127
                offset = SHARE * s - 128 * chunk
                turn = (offset - at) & 127
                spot = lane - offset
                head = spot < 128 - at
                inside = (spot >= 0) & (spot < SHARE) & (spot + done < lengths[s])
                v0 = pltpu.roll(whole[s, pl.ds(pl.multiple_of(here * 8, 8), 8), :], turn, 1)
                v1 = pltpu.roll(whole[s, pl.ds(pl.multiple_of(after * 8, 8), 8), :], turn, 1)
                c0 = jnp.broadcast_to(whole[s, pl.ds(64 + here, 1), :], (8, 128))
                c1 = jnp.broadcast_to(whole[s, pl.ds(64 + after, 1), :], (8, 128))
                c0, c1 = pltpu.roll(c0, turn, 1), pltpu.roll(c1, turn, 1)
                value = jnp.where(inside, jnp.where(head, v0, v1), value)
                cells = jnp.where(inside, jnp.where(head, c0, c1), cells)
            put(chunk, value, cells)

    def finish_round():
        value = vals[...]
        high = value.astype(BF16).astype(F32)
        one_round(code[...] >> 8, code[0:1, :] & 255, high, value - high)

    def block_round(k, carry):
        pl.when(k == 0)(head_of_block)
        pl.when(k == 1)(tail_of_block)
        finish_round()
        return carry

    def beyond_round(k, carry):
        beyond_block(k)
        finish_round()
        return carry

    if block:
        lax.fori_loop(0, jnp.where(most > SHARE, 2, 1), block_round, 0)
    if beyond:
        if fetch is not None:
            pl.when(most > 128)(fetch)
        lax.fori_loop(0, (jnp.maximum(most - 128, 0) + SHARE - 1) // SHARE, beyond_round, 0)


def beside(recv, ch):
    tile = lax.axis_index("tile")
    before, after = jnp.maximum(tile - 1, 0), jnp.minimum(tile + 1, TILES - 1)
    n = KEPT[ch]
    rows = slice(PLACE[ch], PLACE[ch] + 2 * n)
    x = jnp.where(tile == 0, 0.0, recv[before, rows, :])
    y = jnp.where(tile == TILES - 1, 0.0, recv[after, rows, :])
    if n == RIM:
        return x, y
    none = jnp.zeros((RIM - n, 128), F32)
    x = jnp.concatenate([none, x[0:n], none, x[n:]], axis=0)
    return x, jnp.concatenate([y[0:n], none, y[n:], none], axis=0)


def edge_round(ct, a, packed):
    def one_round(row, column, high, low):
        near = row[0:1]
        spot = (near & 31) * 4 + column
        spot = jnp.where(column >= COLS - RIM, spot + (128 - COLS + RIM), spot)
        spot = jnp.where((column < RIM) | (column >= COLS - RIM), spot, -1)
        ct[...] = jnp.where(iota((COLS, DENSE), 0) == spot, 1.0, 0.0).astype(BF16)
        group = row >> 5
        for g in range(GROUPS):
            a[8 * g : 8 * g + 8, :] = jnp.where(group == g, high, 0.0).astype(BF16)
            a[40 + 8 * g : 48 + 8 * g, :] = jnp.where(group == g, low, 0.0).astype(BF16)
        ones = jnp.where(iota((16, DENSE), 0) == group[0:1], 1.0, 0.0)
        a[80:96, :] = ones.astype(BF16)
        got = contract_lanes(a[...], ct[...])
        packed[0:40, :] += (got[0:40] + got[40:80]) * 2.0
        packed[40:48, :] += got[80:88] * 2.0

    return one_round


def edge_body(recv, listed, edge_l, edge_r, flag, vals, code, ct, a, packed):
    most = recv[0, 9:10, :]
    for s in range(1, TILES):
        most = jnp.maximum(most, recv[s, 9:10, :])
    flag[0] = jnp.where(jnp.max(most) > 128.0, 1, 0)
    packed[...] = jnp.zeros(packed.shape, F32)
    scatter(recv, None, vals, code, edge_round(ct, a, packed), beyond=False)
    tails = [x[RIM * h : RIM * h + RIM] for h in (0, 1) for ch in range(4) for x in beside(recv, ch)]
    turned = jnp.transpose(jnp.concatenate(tails + [jnp.zeros((64, 128), F32)], axis=0))
    for side, edge in ((0, edge_l), (1, edge_r)):
        edge[0:48, :] = packed[:, 128 * side : 128 * side + 128]
        for ch in range(4):
            at = LISTED + 8 * ch + RIM * side
            edge[48 + 4 * ch : 52 + 4 * ch, :] = listed[at : at + RIM, :]
        edge[64:68, :] = turned[(128 - RIM) * side : (128 - RIM) * side + RIM]
        edge[68:72, :] = jnp.zeros((4, 128), F32)


def rest_body(recv, whole, old_l, old_r, edge_l, edge_r, vals, code, ct, a, packed):
    packed[:, 0:128] = old_l[0:48, :]
    packed[:, 128:256] = old_r[0:48, :]
    scatter(recv, whole, vals, code, edge_round(ct, a, packed), block=False)
    edge_l[...] = old_l[...]
    edge_r[...] = old_r[...]
    edge_l[0:48, :] = packed[:, 0:128]
    edge_r[0:48, :] = packed[:, 128:256]


def scatter_body(recv, lists, b, w, vals, code, ct, a, hits, whole, arrive):
    b[...] = jnp.zeros(b.shape, F32)
    hits[...] = jnp.zeros(hits.shape, F32)

    def one_round(row, column, high, low):
        ct[...] = jnp.where(iota((COLS, DENSE), 0) == column, 1.0, 0.0).astype(BF16)
        for p in range(4):
            base = p * PIECE
            for i in range(PIECE // 2):
                here = jnp.concatenate([row == base + 2 * i, row == base + 2 * i + 1], axis=0)
                both = jnp.concatenate([high, high], axis=0)
                a[p, 16 * i : 16 * i + 16, :] = jnp.where(here, both, 0.0).astype(BF16)
                both = jnp.concatenate([low, low], axis=0)
                at = 8 * PIECE + 16 * i
                a[p, at : at + 16, :] = jnp.where(here, both, 0.0).astype(BF16)
            ones = jnp.where(iota((48, DENSE), 0) + base == row[0:1], 1.0, 0.0)
            a[p, 16 * PIECE : 16 * PIECE + 48, :] = ones.astype(BF16)
            got = contract_lanes(a[p], ct[...])
            field = (got[: 8 * PIECE] + got[8 * PIECE : 16 * PIECE]) * 2.0
            b[base : base + PIECE] += field.reshape(PIECE, REALS, COLS)
            hits[p] += got[16 * PIECE : 16 * PIECE + 40] * 2.0

    def fetch():
        copy = pltpu.make_async_copy(lists, whole, arrive)
        copy.start()
        copy.wait()

    scatter(recv, whole, vals, code, one_round, fetch=fetch)
    for p in range(4):
        w[PIECE * p : PIECE * p + PIECE, :] = hits[p, 0:PIECE]


def krylov_body(b, w, coef, recv, got_l, got_r, q_out, t_out, moments, own, b3, w3, c3, st, f, q3, from_l, from_r):
    region, tile = lax.axis_index("region"), lax.axis_index("tile")
    from_l[...] = jnp.where(region == 0, 0.0, got_l[...])
    from_r[...] = jnp.where(region == REGIONS - 1, 0.0, got_r[...])
    lane = iota((8, 128), 1)
    at_right, at_left = lane < RIM, lane >= 128 - RIM

    for ref in (b3, f, q3):
        ref[0] = jnp.zeros((REALS, WIDE), F32)
        ref[EXT + 1] = jnp.zeros((REALS, WIDE), F32)

    def east(x):
        return pltpu.roll(x, WIDE - 1, 1)

    def west(x):
        return pltpu.roll(x, 1, 1)

    w3[:, 0:COLS] = w[...]
    for r in range(EXT):
        g, j = r // 32, r % 32
        right, left = from_r[8 * g : 8 * g + 8, :], from_l[8 * g : 8 * g + 8, :]
        right_w, left_w = from_r[40 + g : 41 + g, :], from_l[40 + g : 41 + g, :]
        turn = (128 - 4 * j) % 128
        if turn:
            right, right_w = pltpu.roll(right, turn, 1), pltpu.roll(right_w, turn, 1)
        turn = (252 - 4 * j) % 128
        if turn:
            left, left_w = pltpu.roll(left, turn, 1), pltpu.roll(left_w, turn, 1)
        rim = jnp.where(at_right, right, jnp.where(at_left, left, 0.0))
        b3[r + 1, :, 0:COLS] = b[r]
        b3[r + 1, :, COLS:] = rim
        w3[r : r + 1, COLS:] = jnp.where(
            at_right[0:1], right_w, jnp.where(at_left[0:1], left_w, 0.0)
        )
    c3[:, 0:8, :] = jnp.zeros((4, 8, WIDE), F32)
    c3[:, EXT + 8 :, :] = jnp.zeros((4, 8, WIDE), F32)
    blank = jnp.zeros((128 - 2 * RIM, 128), F32)
    turned = jnp.transpose(jnp.concatenate([from_r[64:68], blank, from_l[64:68]], axis=0))
    own_rows = slice(8 + RIM, 8 + RIM + ROWS)
    for ch in range(4):
        c3[ch, own_rows, 0:COLS] = coef[ch]
        south, north = beside(recv, ch)
        for h in range(2):
            half, cut = slice(RIM * h, RIM * h + RIM), slice(128 * h, 128 * h + 128)
            c3[ch, 8 : 8 + RIM, cut] = south[half]
            c3[ch, 8 + RIM + ROWS : 8 + EXT, cut] = north[half]
        s = slice(48 + 4 * ch, 52 + 4 * ch)
        c3[ch, own_rows, COLS:] = jnp.transpose(jnp.concatenate([from_r[s], blank, from_l[s]], axis=0))
        tail = jnp.where(at_right, turned[8 * ch : 8 * ch + 8], 0.0)
        tail = tail + jnp.where(at_left, turned[32 + 8 * ch : 40 + 8 * ch], 0.0)
        c3[ch, 8 : 8 + RIM, COLS:] = tail[0:RIM]
        c3[ch, 8 + RIM + ROWS : 8 + EXT, COLS:] = tail[RIM : 2 * RIM]

    largest = jnp.ones((8, WIDE), F32)
    for ch in range(4):
        for i in range(EXT // 8):
            largest = jnp.maximum(largest, jnp.abs(c3[ch, 8 + 8 * i : 16 + 8 * i, :]))
    scale = 1.0 / jnp.max(jnp.max(largest, axis=0, keepdims=True), axis=1, keepdims=True)
    w3[...] = w3[...] * (scale * scale)

    lane3 = iota((8, WIDE), 1)
    gx = jnp.where(lane3 >= WIDE - RIM, lane3 - WIDE, lane3) + region * COLS
    here_x = (gx >= 0) & (gx < REGIONS * COLS) & ((lane3 < COLS + RIM) | (lane3 >= WIDE - RIM))
    east_x = here_x & (gx >= 0) & (gx + 1 < REGIONS * COLS) & (lane3 != COLS + RIM - 1)
    st[:, 0:1, :] = jnp.zeros((5, 1, WIDE), F32)
    st[:, EXT + 1 : EXT + 2, :] = jnp.zeros((5, 1, WIDE), F32)
    for i in range(EXT // 8):
        at = 8 + 8 * i
        gy = tile * ROWS - RIM + 8 * i + iota((8, WIDE), 0)
        here_y = (gy >= 0) & (gy < TILES * ROWS)
        north_y = (gy >= 0) & (gy + 1 < TILES * ROWS)
        south_y = (gy >= 1) & (gy < TILES * ROWS)

        def near(ch, dy):
            x = c3[ch, at : at + 8, :]
            if dy == 1:
                x = jnp.concatenate([x[1:8], c3[ch, at + 8 : at + 16, :][0:1]], axis=0)
            if dy == -1:
                x = jnp.concatenate([c3[ch, at - 8 : at, :][7:8], x[0:7]], axis=0)
            return x

        h11, h22, mixed = near(0, 0), near(1, 0), near(2, 0)
        e, wst = 0.5 * (east(h11) + h11), 0.5 * (west(h11) + h11)
        n, s = 0.5 * (near(1, 1) + h22), 0.5 * (near(1, -1) + h22)
        rows = slice(8 * i + 1, 8 * i + 9)
        side = east(mixed)
        st[0, rows, :] = jnp.where(here_x & here_y, scale * (near(3, 0) + ((e + wst) + (n + s))), 0.0)
        st[1, rows, :] = jnp.where(east_x & here_y, -scale * e, 0.0)
        st[2, rows, :] = jnp.where(here_x & north_y, -scale * n, 0.0)
        st[3, rows, :] = jnp.where(east_x & north_y, (-0.25 * scale) * (side + near(2, 1)), 0.0)
        st[4, rows, :] = jnp.where(east_x & south_y, (0.25 * scale) * (side + near(2, -1)), 0.0)

    def apply(src, start, count, finish, put):
        def cells(r):
            x = src[r + 1]
            return x, east(x), [st[k, r + 1 : r + 2, :] for k in range(5)]

        below, here = cells(start - 1), cells(start)
        for r in range(start, start + count):
            above = cells(r + 1)
            (v0, e0, c0), (v1, e1, c1), (v2, e2, c2) = below, here, above
            from_west = c1[1] * v1 + c0[3] * v0 + c2[4] * v2
            total = c1[0] * v1 + c1[1] * e1 + c1[2] * v2 + c0[2] * v0
            total = total + (c1[3] * e2 + c1[4] * e0) + west(from_west)
            put(r, finish(r, total))
            below, here = here, above

    def plain(r, total):
        return total

    def with_b(r, total):
        return PREC_SCALE * total + w3[pl.ds(r, 1), :] * b3[r + 1]

    sums = [jnp.zeros((REALS, COLS), F32) for _ in range(3)]

    def with_q(r, total):
        q = q3[r + 1, :, 0:COLS]
        x = b3[r + 1, :, 0:COLS]
        t = PREC_SCALE * total[:, :COLS] + w3[pl.ds(r, 1), 0:COLS] * q
        sums[:] = [sums[0] + x * x, sums[1] + x * q, sums[2] + x * t]
        return q, t

    def put_f(r, x):
        f[r + 1] = x

    def put_q(r, x):
        q3[r + 1] = x

    def put_t(r, x):
        q_out[r - RIM] = x[0]
        t_out[r - RIM] = x[1]

    apply(b3, 1, EXT - 2, plain, put_f)
    apply(f, 2, EXT - 4, with_b, put_q)
    apply(q3, 3, EXT - 6, plain, put_f)
    apply(f, RIM, ROWS, with_q, put_t)

    def total(x):
        return jnp.sum(x, axis=1, keepdims=True)

    bb, bq, bt = [total(x) for x in sums]
    safe = jnp.where(bb > 0.0, bb, 1.0)
    sigma, tau = bq / safe, bt / safe

    def second(i, acc):
        uu, uz = acc
        for d in range(8):
            r = 8 * i + d
            x = b[r + RIM]
            u = q_out[r] - sigma * x
            uu, uz = uu + u * u, uz + u * (t_out[r] - tau * x)
        return uu, uz

    zero = jnp.zeros((REALS, COLS), F32)
    uu, uz = [total(x) for x in lax.fori_loop(0, ROWS // 8, second, (zero, zero))]
    mu = uz / jnp.where(uu > 0.0, uu, 1.0)
    inverse = 1.0 / (scale * scale)
    own[...] = jnp.broadcast_to(inverse, (8, 128))
    column = [jnp.broadcast_to(x, (8, 128)) for x in (bb, sigma, uu, tau, mu, inverse)]
    moments[...] = jnp.transpose(jnp.concatenate(column + [jnp.zeros((80, 128), F32)], axis=0))


def finish_body(moments, own, b, q, t, x_out, r_out, x_own, r_own, leave):
    turned = jnp.transpose(moments[...])
    bb, sigma, uu, tau, mu, inverse = [turned[8 * m : 8 * m + 8] for m in range(6)]

    def total(x):
        return jnp.sum(x, axis=1, keepdims=True)

    norm0 = total(bb)
    alpha0 = norm0 / total(bb * sigma * inverse)
    a = alpha0 * inverse
    off = 1.0 - a * sigma
    norm1 = total(off * off * bb + a * a * uu)
    beta = norm1 / norm0
    grow = 1.0 + beta
    along = (grow - a * sigma) * (grow * sigma - a * tau) * bb
    curve = total(inverse * (along - a * (grow - a * mu) * uu))
    alpha1 = norm1 / curve
    mine = own[:, 0:1]
    a0 = alpha0 * mine
    a1 = alpha1 * mine

    copies = []
    for i in range(ROWS // PART):
        for r in range(PART * i, PART * i + PART):
            x, y, z = b[r + RIM], q[r], t[r]
            r1 = x - a0 * y
            d1 = r1 + beta * x
            x_own[r] = alpha0 * x + alpha1 * d1
            r_own[r] = r1 - a1 * (grow * y - a0 * z)
        rows = pl.ds(PART * i, PART)
        copies.append(pltpu.make_async_copy(x_own.at[rows], x_out.at[rows], leave.at[0, i]))
        copies.append(pltpu.make_async_copy(r_own.at[rows], r_out.at[rows], leave.at[1, i]))
        for c in copies[-2:]:
            c.start()
    for c in copies:
        c.wait()


def call(body, shapes, scratch, *args, ins=None, outs=None, limit=VMEM_LIMIT, cost=None, types=None):
    ins = ins or [pltpu.VMEM] * len(args)
    outs = outs or [pltpu.VMEM] * len(shapes)
    return pl.pallas_call(
        body,
        out_shape=[
            jax.ShapeDtypeStruct(s, t) for s, t in zip(shapes, types or [F32] * len(shapes))
        ],
        in_specs=[pl.BlockSpec(memory_space=m) for m in ins],
        out_specs=[pl.BlockSpec(memory_space=m) for m in outs],
        scratch_shapes=scratch,
        compiler_params=pltpu.CompilerParams(vmem_limit_bytes=limit),
        cost_estimate=cost,
    )(*args)


def local(coeffs, obs_cell, obs_value, obs_count):
    def ring(x, axis, size, step):
        return lax.ppermute(x, axis, [(i, (i + step) % size) for i in range(size)])

    packed, listed, space = call(
        sort_body,
        [(TILES, MESSAGE, 128), (LISTED + 32, 128), (TILES, LISTED, 128)],
        [
            pltpu.VMEM((1, SLOTS), I32),
            pltpu.VMEM((REALS, SLOTS), F32),
            pltpu.VMEM((4, ROWS, COLS), F32),
            pltpu.SemaphoreType.DMA((3,)),
        ],
        obs_count,
        obs_cell.reshape(1, SLOTS),
        obs_value,
        coeffs,
        ins=[pltpu.SMEM, pltpu.HBM, pltpu.HBM, pltpu.HBM],
        outs=[pltpu.VMEM, pltpu.VMEM, pltpu.HBM],
        limit=60 * 1024 * 1024,
    )
    recv = lax.all_to_all(packed, "tile", 0, 0)

    work = [
        pltpu.VMEM((REALS, DENSE), F32),
        pltpu.VMEM((REALS, DENSE), I32),
        pltpu.VMEM((COLS, DENSE), BF16),
        pltpu.VMEM((96, DENSE), BF16),
        pltpu.VMEM((48, COLS), F32),
    ]
    sides = [(72, 128), (72, 128)]
    edge_l, edge_r, flag = call(
        edge_body,
        sides + [(1,)],
        work,
        recv,
        listed,
        outs=[pltpu.VMEM, pltpu.VMEM, pltpu.SMEM],
        types=[F32, F32, I32],
    )

    def share(recv, listed, space, edge_l, edge_r):
        whole = jnp.broadcast_to(listed[None, :LISTED], (TILES, LISTED, 128))
        whole = lax.all_to_all(whole, "tile", 0, 0)
        return (whole, *call(rest_body, sides, work, recv, whole, edge_l, edge_r))

    def skip(recv, listed, space, edge_l, edge_r):
        return space, edge_l, edge_r

    whole, edge_l, edge_r = lax.cond(flag[0] > 0, share, skip, recv, listed, space, edge_l, edge_r)
    b, w = call(
        scatter_body,
        [(EXT, REALS, COLS), (EXT, COLS)],
        [
            pltpu.VMEM((REALS, DENSE), F32),
            pltpu.VMEM((REALS, DENSE), I32),
            pltpu.VMEM((COLS, DENSE), BF16),
            pltpu.VMEM((4, 16 * PIECE + 48, DENSE), BF16),
            pltpu.VMEM((4, 40, COLS), F32),
            pltpu.VMEM((TILES, LISTED, 128), F32),
            pltpu.SemaphoreType.DMA,
        ],
        recv,
        whole,
        ins=[pltpu.VMEM, pltpu.HBM],
        cost=pl.CostEstimate(flops=2 * 2368 * DENSE * COLS, bytes_accessed=1 << 23, transcendentals=0),
    )
    from_l = ring(edge_r, "region", REGIONS, 1)
    from_r = ring(edge_l, "region", REGIONS, -1)
    field = (ROWS, REALS, COLS)
    q, t, moments, own = call(
        krylov_body,
        [field, field, (128, 128), (8, 128)],
        [
            pltpu.VMEM((EXT + 2, REALS, WIDE), F32),
            pltpu.VMEM((EXT, WIDE), F32),
            pltpu.VMEM((4, EXT + 16, WIDE), F32),
            pltpu.VMEM((5, EXT + 2, WIDE), F32),
            pltpu.VMEM((EXT + 2, REALS, WIDE), F32),
            pltpu.VMEM((EXT + 2, REALS, WIDE), F32),
            pltpu.VMEM((72, 128), F32),
            pltpu.VMEM((72, 128), F32),
        ],
        b,
        w,
        coeffs,
        recv,
        from_l,
        from_r,
    )
    shared = lax.all_to_all(moments, ("region", "tile"), 0, 0, tiled=True)
    return tuple(
        call(
            finish_body,
            [field, field],
            [
                pltpu.VMEM(field, F32),
                pltpu.VMEM(field, F32),
                pltpu.SemaphoreType.DMA((2, ROWS // PART)),
            ],
            shared,
            own,
            b,
            q,
            t,
            outs=[pltpu.HBM, pltpu.HBM],
        )
    )


def solution(mesh):
    placed = (
        P(None, "tile", "region"),
        P(("region", "tile")),
        P(None, ("region", "tile")),
        P(("region", "tile")),
    )
    return jax.shard_map(
        local,
        mesh=mesh,
        in_specs=placed,
        out_specs=(P("tile", None, "region"), P("tile", None, "region")),
        check_vma=False,
    )
```

```python
import jax
import jax.numpy as jnp
from jax import lax
from jax.experimental import pallas as pl
from jax.experimental.pallas import tpu as pltpu
from jax.sharding import PartitionSpec as P

PREC_SCALE = 0.01
RIM = 4
ROWS, COLS = 128, 256
REALS = 8
SLOTS = 1024
TILES, REGIONS = 16, 8
EXT = ROWS + 2 * RIM
MESSAGE = 40
LISTED = 72
PLACE = (32, 16, 24, 10)
KEPT = (3, 4, 4, 3)
DEAD = 4096 * 256
WIDE = COLS + 128
CHUNKS = SLOTS // 128
SHARE = 96
DENSE = TILES * SHARE
GROUPS = 5
PART = 32
PIECE = EXT // 4
F32, BF16, I32 = jnp.float32, jnp.bfloat16, jnp.int32
VMEM_LIMIT = 48 * 1024 * 1024


def iota(shape, dim):
    return lax.broadcasted_iota(I32, shape, dim)


def contract_lanes(a, b):
    return lax.dot_general(a, b, (((1,), (1,)), ((), ())), preferred_element_type=F32)


def sort_body(count, cell_hbm, value_hbm, coef_hbm, out, listed, space, cell_ref, value_ref, coef, arrive):
    copies = [
        pltpu.make_async_copy(cell_hbm, cell_ref, arrive.at[0]),
        pltpu.make_async_copy(value_hbm, value_ref, arrive.at[1]),
        pltpu.make_async_copy(coef_hbm, coef, arrive.at[2]),
    ]
    for c in copies:
        c.start()
    copies[0].wait()
    cell = cell_ref[...]
    index = iota((1, SLOTS), 1)
    live = index < count[0]
    key = (jnp.where(live, cell >> 8, 4096) * SLOTS + index).astype(F32)
    tall = jnp.transpose(jnp.broadcast_to(key, (128, SLOTS)))
    across = [jnp.broadcast_to(key[:, 128 * i : 128 * i + 128], (8, 128)) for i in range(CHUNKS)]
    below = [jnp.zeros((8, 128), F32) for _ in range(CHUNKS)]
    for j in range(SLOTS // 8):
        column = tall[8 * j : 8 * j + 8]
        for i in range(CHUNKS):
            below[i] = below[i] + jnp.where(column < across[i], 1.0, 0.0)
    rank = jnp.concatenate([jnp.sum(x, axis=0, keepdims=True) for x in below], axis=1).astype(I32)
    code = jnp.where(live, cell, DEAD)
    copies[1].wait()
    value = value_ref[...]
    top = value.astype(BF16).astype(F32)
    rest = value - top
    middle = rest.astype(BF16).astype(F32)
    left = jnp.concatenate(
        [
            top,
            middle,
            rest - middle,
            (code & 255).astype(F32),
            ((code >> 8) & 255).astype(F32),
            (code >> 16).astype(F32),
            jnp.zeros((5, SLOTS), F32),
        ],
        axis=0,
    ).astype(BF16)
    for k in range(SLOTS // 256):
        spot = jnp.where(iota((256, SLOTS), 0) + 256 * k == rank, 1.0, 0.0).astype(BF16)
        moved = contract_lanes(left, spot)
        values = (moved[0:8] + moved[8:16]) + moved[16:24]
        codes = moved[24:25] + 256.0 * moved[25:26] + 65536.0 * moved[26:27]
        for h in range(2):
            c = 2 * k + h
            listed[8 * c : 8 * c + 8, :] = values[:, 128 * h : 128 * h + 128]
            listed[64 + c : 65 + c, :] = codes[:, 128 * h : 128 * h + 128]
    cells = listed[64:72, :]
    lane = iota((1, 128), 1)
    starts, lengths = [], []
    for s in range(TILES):
        edge = [float((ROWS * s - RIM) * COLS), float((ROWS * s + ROWS + RIM) * COLS)]
        start, end = [jnp.sum(jnp.where(cells < x, 1.0, 0.0)).astype(I32) for x in edge]
        starts.append(start)
        lengths.append(end - start)
    most = lengths[0]
    for x in lengths[1:]:
        most = jnp.maximum(most, x)
    for s in range(TILES):
        here = jnp.minimum(starts[s] >> 7, CHUNKS - 1)
        after = jnp.minimum(here + 1, CHUNKS - 1)
        at = starts[s] & 127
        turn = (128 - at) & 127
        head = lane < 128 - at
        v0 = pltpu.roll(listed[pl.ds(pl.multiple_of(here * 8, 8), 8), :], turn, 1)
        v1 = pltpu.roll(listed[pl.ds(pl.multiple_of(after * 8, 8), 8), :], turn, 1)
        c0 = pltpu.roll(listed[pl.ds(64 + here, 1), :], turn, 1)
        c1 = pltpu.roll(listed[pl.ds(64 + after, 1), :], turn, 1)
        out[s, 0:8, :] = jnp.where(head, v0, v1)
        out[s, 8:9, :] = jnp.where(lane < lengths[s], jnp.where(head, c0, c1), float(DEAD))
        counts = jnp.where(lane < 64, most.astype(F32), lengths[s].astype(F32))
        out[s, 9:10, :] = counts
        out[s, 38:40, :] = jnp.zeros((2, 128), F32)
    copies[2].wait()
    tile = lax.axis_index("tile")
    for ch in range(4):
        n = KEPT[ch]
        x, y = coef[ch, 0:n, :], coef[ch, ROWS - n : ROWS, :]
        x = jnp.concatenate([x[:, 0:128], x[:, 128:256]], axis=0)
        y = jnp.concatenate([y[:, 0:128], y[:, 128:256]], axis=0)
        for s in range(TILES):
            out[s, PLACE[ch] : PLACE[ch] + 2 * n, :] = jnp.where(tile + 1 == s, y, x)
        at = LISTED + 8 * ch
        listed[at : at + RIM, :] = jnp.transpose(coef[ch, :, 0:128])[0:RIM]
        listed[at + RIM : at + 8, :] = jnp.transpose(coef[ch, :, 128:256])[128 - RIM : 128]


def scatter(recv, whole, vals, code, one_round, block=True, beyond=True, fetch=None):
    first = lax.axis_index("tile") * ROWS - RIM
    lane = iota((1, 128), 1)
    most = recv[0, 9:10, :]
    for s in range(1, TILES):
        most = jnp.maximum(most, recv[s, 9:10, :])
    most = jnp.max(jnp.where(lane < 64, 0.0, most)).astype(I32)

    def put(chunk, value, cells):
        vals[:, 128 * chunk : 128 * chunk + 128] = value
        code[:, 128 * chunk : 128 * chunk + 128] = cells.astype(I32) - first * COLS

    def blank():
        return jnp.zeros((REALS, 128), F32), jnp.full((8, 128), float(DEAD), F32)

    def head_of_block():
        for chunk in range(DENSE // 128):
            value, cells = blank()
            for s in range(128 * chunk // SHARE, (128 * chunk + 127) // SHARE + 1):
                offset = SHARE * s - 128 * chunk
                x, y = recv[s, 0:8, :], jnp.broadcast_to(recv[s, 8:9, :], (8, 128))
                if offset % 128:
                    x, y = pltpu.roll(x, offset % 128, 1), pltpu.roll(y, offset % 128, 1)
                inside = (lane >= offset) & (lane < offset + SHARE)
                value, cells = jnp.where(inside, x, value), jnp.where(inside, y, cells)
            put(chunk, value, cells)

    def tail_of_block():
        each = 128 - SHARE
        per = 128 // each
        for chunk in range(DENSE // 128):
            value, cells = blank()
            for s in range(per * chunk, min(per * chunk + per, TILES)):
                offset = each * (s % per)
                turn = (offset - SHARE) % 128
                x = pltpu.roll(recv[s, 0:8, :], turn, 1)
                y = pltpu.roll(jnp.broadcast_to(recv[s, 8:9, :], (8, 128)), turn, 1)
                inside = (lane >= offset) & (lane < offset + each)
                value, cells = jnp.where(inside, x, value), jnp.where(inside, y, cells)
            put(chunk, value, cells)

    def beyond_block(k):
        low_cell = (first * COLS).astype(F32)
        high_cell = ((first + EXT) * COLS).astype(F32)
        starts, lengths = [], []
        for s in range(TILES):
            cells = whole[s, 64:72, :]
            start = jnp.sum(jnp.where(cells < low_cell, 1.0, 0.0)).astype(I32)
            end = jnp.sum(jnp.where(cells < high_cell, 1.0, 0.0)).astype(I32)
            starts.append(start)
            lengths.append(end - start)
        done = 128 + SHARE * k
        for chunk in range(DENSE // 128):
            value, cells = blank()
            for s in range(128 * chunk // SHARE, (128 * chunk + 127) // SHARE + 1):
                begin = starts[s] + done
                here = jnp.minimum(begin >> 7, CHUNKS - 1)
                after = jnp.minimum(here + 1, CHUNKS - 1)
                at = begin & 127
                offset = SHARE * s - 128 * chunk
                turn = (offset - at) & 127
                spot = lane - offset
                head = spot < 128 - at
                inside = (spot >= 0) & (spot < SHARE) & (spot + done < lengths[s])
                v0 = pltpu.roll(whole[s, pl.ds(pl.multiple_of(here * 8, 8), 8), :], turn, 1)
                v1 = pltpu.roll(whole[s, pl.ds(pl.multiple_of(after * 8, 8), 8), :], turn, 1)
                c0 = jnp.broadcast_to(whole[s, pl.ds(64 + here, 1), :], (8, 128))
                c1 = jnp.broadcast_to(whole[s, pl.ds(64 + after, 1), :], (8, 128))
                c0, c1 = pltpu.roll(c0, turn, 1), pltpu.roll(c1, turn, 1)
                value = jnp.where(inside, jnp.where(head, v0, v1), value)
                cells = jnp.where(inside, jnp.where(head, c0, c1), cells)
            put(chunk, value, cells)

    def finish_round():
        value = vals[...]
        high = value.astype(BF16).astype(F32)
        one_round(code[...] >> 8, code[0:1, :] & 255, high, value - high)

    def block_round(k, carry):
        pl.when(k == 0)(head_of_block)
        pl.when(k == 1)(tail_of_block)
        finish_round()
        return carry

    def beyond_round(k, carry):
        beyond_block(k)
        finish_round()
        return carry

    if block:
        lax.fori_loop(0, jnp.where(most > SHARE, 2, 1), block_round, 0)
    if beyond:
        if fetch is not None:
            pl.when(most > 128)(fetch)
        lax.fori_loop(0, (jnp.maximum(most - 128, 0) + SHARE - 1) // SHARE, beyond_round, 0)


def beside(recv, ch):
    tile = lax.axis_index("tile")
    before, after = jnp.maximum(tile - 1, 0), jnp.minimum(tile + 1, TILES - 1)
    n = KEPT[ch]
    rows = slice(PLACE[ch], PLACE[ch] + 2 * n)
    x = jnp.where(tile == 0, 0.0, recv[before, rows, :])
    y = jnp.where(tile == TILES - 1, 0.0, recv[after, rows, :])
    if n == RIM:
        return x, y
    none = jnp.zeros((RIM - n, 128), F32)
    x = jnp.concatenate([none, x[0:n], none, x[n:]], axis=0)
    return x, jnp.concatenate([y[0:n], none, y[n:], none], axis=0)


def edge_round(ct, a, packed):
    def one_round(row, column, high, low):
        near = row[0:1]
        spot = (near & 31) * 4 + column
        spot = jnp.where(column >= COLS - RIM, spot + (128 - COLS + RIM), spot)
        spot = jnp.where((column < RIM) | (column >= COLS - RIM), spot, -1)
        ct[...] = jnp.where(iota((COLS, DENSE), 0) == spot, 1.0, 0.0).astype(BF16)
        group = row >> 5
        for g in range(GROUPS):
            a[8 * g : 8 * g + 8, :] = jnp.where(group == g, high, 0.0).astype(BF16)
            a[40 + 8 * g : 48 + 8 * g, :] = jnp.where(group == g, low, 0.0).astype(BF16)
        ones = jnp.where(iota((16, DENSE), 0) == group[0:1], 1.0, 0.0)
        a[80:96, :] = ones.astype(BF16)
        got = contract_lanes(a[...], ct[...])
        packed[0:40, :] += (got[0:40] + got[40:80]) * 2.0
        packed[40:48, :] += got[80:88] * 2.0

    return one_round


def edge_body(recv, listed, edge_l, edge_r, flag, vals, code, ct, a, packed):
    most = recv[0, 9:10, :]
    for s in range(1, TILES):
        most = jnp.maximum(most, recv[s, 9:10, :])
    flag[0] = jnp.where(jnp.max(most) > 128.0, 1, 0)
    packed[...] = jnp.zeros(packed.shape, F32)
    scatter(recv, None, vals, code, edge_round(ct, a, packed), beyond=False)
    tails = [x[RIM * h : RIM * h + RIM] for h in (0, 1) for ch in range(4) for x in beside(recv, ch)]
    turned = jnp.transpose(jnp.concatenate(tails + [jnp.zeros((64, 128), F32)], axis=0))
    for side, edge in ((0, edge_l), (1, edge_r)):
        edge[0:48, :] = packed[:, 128 * side : 128 * side + 128]
        for ch in range(4):
            at = LISTED + 8 * ch + RIM * side
            edge[48 + 4 * ch : 52 + 4 * ch, :] = listed[at : at + RIM, :]
        edge[64:68, :] = turned[(128 - RIM) * side : (128 - RIM) * side + RIM]
        edge[68:72, :] = jnp.zeros((4, 128), F32)


def rest_body(recv, whole, old_l, old_r, edge_l, edge_r, vals, code, ct, a, packed):
    packed[:, 0:128] = old_l[0:48, :]
    packed[:, 128:256] = old_r[0:48, :]
    scatter(recv, whole, vals, code, edge_round(ct, a, packed), block=False)
    edge_l[...] = old_l[...]
    edge_r[...] = old_r[...]
    edge_l[0:48, :] = packed[:, 0:128]
    edge_r[0:48, :] = packed[:, 128:256]


def scatter_body(recv, lists, b, w, vals, code, ct, a, hits, whole, arrive):
    b[...] = jnp.zeros(b.shape, F32)
    hits[...] = jnp.zeros(hits.shape, F32)

    def one_round(row, column, high, low):
        ct[...] = jnp.where(iota((COLS, DENSE), 0) == column, 1.0, 0.0).astype(BF16)
        for p in range(4):
            base = p * PIECE
            for i in range(PIECE // 2):
                here = jnp.concatenate([row == base + 2 * i, row == base + 2 * i + 1], axis=0)
                both = jnp.concatenate([high, high], axis=0)
                a[p, 16 * i : 16 * i + 16, :] = jnp.where(here, both, 0.0).astype(BF16)
                both = jnp.concatenate([low, low], axis=0)
                at = 8 * PIECE + 16 * i
                a[p, at : at + 16, :] = jnp.where(here, both, 0.0).astype(BF16)
            ones = jnp.where(iota((48, DENSE), 0) + base == row[0:1], 1.0, 0.0)
            a[p, 16 * PIECE : 16 * PIECE + 48, :] = ones.astype(BF16)
            got = contract_lanes(a[p], ct[...])
            field = (got[: 8 * PIECE] + got[8 * PIECE : 16 * PIECE]) * 2.0
            b[base : base + PIECE] += field.reshape(PIECE, REALS, COLS)
            hits[p] += got[16 * PIECE : 16 * PIECE + 40] * 2.0

    def fetch():
        copy = pltpu.make_async_copy(lists, whole, arrive)
        copy.start()
        copy.wait()

    scatter(recv, whole, vals, code, one_round, fetch=fetch)
    for p in range(4):
        w[PIECE * p : PIECE * p + PIECE, :] = hits[p, 0:PIECE]


def krylov_body(b, w, coef, recv, got_l, got_r, q_out, t_out, moments, own, b3, w3, c3, st, f, q3, from_l, from_r):
    region, tile = lax.axis_index("region"), lax.axis_index("tile")
    from_l[...] = jnp.where(region == 0, 0.0, got_l[...])
    from_r[...] = jnp.where(region == REGIONS - 1, 0.0, got_r[...])
    lane = iota((8, 128), 1)
    at_right, at_left = lane < RIM, lane >= 128 - RIM

    for ref in (b3, f, q3):
        ref[0] = jnp.zeros((REALS, WIDE), F32)
        ref[EXT + 1] = jnp.zeros((REALS, WIDE), F32)

    def east(x):
        return pltpu.roll(x, WIDE - 1, 1)

    def west(x):
        return pltpu.roll(x, 1, 1)

    w3[:, 0:COLS] = w[...]
    for r in range(EXT):
        g, j = r // 32, r % 32
        right, left = from_r[8 * g : 8 * g + 8, :], from_l[8 * g : 8 * g + 8, :]
        right_w, left_w = from_r[40 + g : 41 + g, :], from_l[40 + g : 41 + g, :]
        turn = (128 - 4 * j) % 128
        if turn:
            right, right_w = pltpu.roll(right, turn, 1), pltpu.roll(right_w, turn, 1)
        turn = (252 - 4 * j) % 128
        if turn:
            left, left_w = pltpu.roll(left, turn, 1), pltpu.roll(left_w, turn, 1)
        rim = jnp.where(at_right, right, jnp.where(at_left, left, 0.0))
        b3[r + 1, :, 0:COLS] = b[r]
        b3[r + 1, :, COLS:] = rim
        w3[r : r + 1, COLS:] = jnp.where(
            at_right[0:1], right_w, jnp.where(at_left[0:1], left_w, 0.0)
        )
    c3[:, 0:8, :] = jnp.zeros((4, 8, WIDE), F32)
    c3[:, EXT + 8 :, :] = jnp.zeros((4, 8, WIDE), F32)
    blank = jnp.zeros((128 - 2 * RIM, 128), F32)
    turned = jnp.transpose(jnp.concatenate([from_r[64:68], blank, from_l[64:68]], axis=0))
    own_rows = slice(8 + RIM, 8 + RIM + ROWS)
    for ch in range(4):
        c3[ch, own_rows, 0:COLS] = coef[ch]
        south, north = beside(recv, ch)
        for h in range(2):
            half, cut = slice(RIM * h, RIM * h + RIM), slice(128 * h, 128 * h + 128)
            c3[ch, 8 : 8 + RIM, cut] = south[half]
            c3[ch, 8 + RIM + ROWS : 8 + EXT, cut] = north[half]
        s = slice(48 + 4 * ch, 52 + 4 * ch)
        c3[ch, own_rows, COLS:] = jnp.transpose(jnp.concatenate([from_r[s], blank, from_l[s]], axis=0))
        tail = jnp.where(at_right, turned[8 * ch : 8 * ch + 8], 0.0)
        tail = tail + jnp.where(at_left, turned[32 + 8 * ch : 40 + 8 * ch], 0.0)
        c3[ch, 8 : 8 + RIM, COLS:] = tail[0:RIM]
        c3[ch, 8 + RIM + ROWS : 8 + EXT, COLS:] = tail[RIM : 2 * RIM]

    largest = jnp.ones((8, WIDE), F32)
    for ch in range(4):
        for i in range(EXT // 8):
            largest = jnp.maximum(largest, jnp.abs(c3[ch, 8 + 8 * i : 16 + 8 * i, :]))
    scale = 1.0 / jnp.max(jnp.max(largest, axis=0, keepdims=True), axis=1, keepdims=True)
    w3[...] = w3[...] * (scale * scale)

    lane3 = iota((8, WIDE), 1)
    gx = jnp.where(lane3 >= WIDE - RIM, lane3 - WIDE, lane3) + region * COLS
    here_x = (gx >= 0) & (gx < REGIONS * COLS) & ((lane3 < COLS + RIM) | (lane3 >= WIDE - RIM))
    east_x = here_x & (gx >= 0) & (gx + 1 < REGIONS * COLS) & (lane3 != COLS + RIM - 1)
    st[:, 0:1, :] = jnp.zeros((5, 1, WIDE), F32)
    st[:, EXT + 1 : EXT + 2, :] = jnp.zeros((5, 1, WIDE), F32)
    for i in range(EXT // 8):
        at = 8 + 8 * i
        gy = tile * ROWS - RIM + 8 * i + iota((8, WIDE), 0)
        here_y = (gy >= 0) & (gy < TILES * ROWS)
        north_y = (gy >= 0) & (gy + 1 < TILES * ROWS)
        south_y = (gy >= 1) & (gy < TILES * ROWS)

        def near(ch, dy):
            x = c3[ch, at : at + 8, :]
            if dy == 1:
                x = jnp.concatenate([x[1:8], c3[ch, at + 8 : at + 16, :][0:1]], axis=0)
            if dy == -1:
                x = jnp.concatenate([c3[ch, at - 8 : at, :][7:8], x[0:7]], axis=0)
            return x

        h11, h22, mixed = near(0, 0), near(1, 0), near(2, 0)
        e, wst = 0.5 * (east(h11) + h11), 0.5 * (west(h11) + h11)
        n, s = 0.5 * (near(1, 1) + h22), 0.5 * (near(1, -1) + h22)
        rows = slice(8 * i + 1, 8 * i + 9)
        side = east(mixed)
        st[0, rows, :] = jnp.where(here_x & here_y, scale * (near(3, 0) + ((e + wst) + (n + s))), 0.0)
        st[1, rows, :] = jnp.where(east_x & here_y, -scale * e, 0.0)
        st[2, rows, :] = jnp.where(here_x & north_y, -scale * n, 0.0)
        st[3, rows, :] = jnp.where(east_x & north_y, (-0.25 * scale) * (side + near(2, 1)), 0.0)
        st[4, rows, :] = jnp.where(east_x & south_y, (0.25 * scale) * (side + near(2, -1)), 0.0)

    def apply(src, start, count, finish, put):
        def cells(r):
            x = src[r + 1]
            return x, east(x), [st[k, r + 1 : r + 2, :] for k in range(5)]

        below, here = cells(start - 1), cells(start)
        for r in range(start, start + count):
            above = cells(r + 1)
            (v0, e0, c0), (v1, e1, c1), (v2, e2, c2) = below, here, above
            from_west = c1[1] * v1 + c0[3] * v0 + c2[4] * v2
            total = c1[0] * v1 + c1[1] * e1 + c1[2] * v2 + c0[2] * v0
            total = total + (c1[3] * e2 + c1[4] * e0) + west(from_west)
            put(r, finish(r, total))
            below, here = here, above

    def plain(r, total):
        return total

    def with_b(r, total):
        return PREC_SCALE * total + w3[pl.ds(r, 1), :] * b3[r + 1]

    sums = [jnp.zeros((REALS, COLS), F32) for _ in range(3)]

    def with_q(r, total):
        q = q3[r + 1, :, 0:COLS]
        x = b3[r + 1, :, 0:COLS]
        t = PREC_SCALE * total[:, :COLS] + w3[pl.ds(r, 1), 0:COLS] * q
        sums[:] = [sums[0] + x * x, sums[1] + x * q, sums[2] + x * t]
        return q, t

    def put_f(r, x):
        f[r + 1] = x

    def put_q(r, x):
        q3[r + 1] = x

    def put_t(r, x):
        q_out[r - RIM] = x[0]
        t_out[r - RIM] = x[1]

    apply(b3, 1, EXT - 2, plain, put_f)
    apply(f, 2, EXT - 4, with_b, put_q)
    apply(q3, 3, EXT - 6, plain, put_f)
    apply(f, RIM, ROWS, with_q, put_t)

    def total(x):
        return jnp.sum(x, axis=1, keepdims=True)

    bb, bq, bt = [total(x) for x in sums]
    safe = jnp.where(bb > 0.0, bb, 1.0)
    sigma, tau = bq / safe, bt / safe

    def second(i, acc):
        uu, uz = acc
        for d in range(8):
            r = 8 * i + d
            x = b[r + RIM]
            u = q_out[r] - sigma * x
            uu, uz = uu + u * u, uz + u * (t_out[r] - tau * x)
        return uu, uz

    zero = jnp.zeros((REALS, COLS), F32)
    uu, uz = [total(x) for x in lax.fori_loop(0, ROWS // 8, second, (zero, zero))]
    mu = uz / jnp.where(uu > 0.0, uu, 1.0)
    inverse = 1.0 / (scale * scale)
    own[...] = jnp.broadcast_to(inverse, (8, 128))
    column = [jnp.broadcast_to(x, (8, 128)) for x in (bb, sigma, uu, tau, mu, inverse)]
    moments[...] = jnp.transpose(jnp.concatenate(column + [jnp.zeros((80, 128), F32)], axis=0))


def finish_body(moments, own, b, q, t, x_out, r_out, x_own, r_own, leave):
    turned = jnp.transpose(moments[...])
    bb, sigma, uu, tau, mu, inverse = [turned[8 * m : 8 * m + 8] for m in range(6)]

    def total(x):
        return jnp.sum(x, axis=1, keepdims=True)

    norm0 = total(bb)
    alpha0 = norm0 / total(bb * sigma * inverse)
    a = alpha0 * inverse
    off = 1.0 - a * sigma
    norm1 = total(off * off * bb + a * a * uu)
    beta = norm1 / norm0
    grow = 1.0 + beta
    along = (grow - a * sigma) * (grow * sigma - a * tau) * bb
    curve = total(inverse * (along - a * (grow - a * mu) * uu))
    alpha1 = norm1 / curve
    mine = own[:, 0:1]
    a0 = alpha0 * mine
    a1 = alpha1 * mine

    copies = []
    for i in range(ROWS // PART):
        for r in range(PART * i, PART * i + PART):
            x, y, z = b[r + RIM], q[r], t[r]
            r1 = x - a0 * y
            d1 = r1 + beta * x
            x_own[r] = alpha0 * x + alpha1 * d1
            r_own[r] = r1 - a1 * (grow * y - a0 * z)
        rows = pl.ds(PART * i, PART)
        copies.append(pltpu.make_async_copy(x_own.at[rows], x_out.at[rows], leave.at[0, i]))
        copies.append(pltpu.make_async_copy(r_own.at[rows], r_out.at[rows], leave.at[1, i]))
        for c in copies[-2:]:
            c.start()
    for c in copies:
        c.wait()


def call(body, shapes, scratch, *args, ins=None, outs=None, limit=VMEM_LIMIT, cost=None, types=None):
    ins = ins or [pltpu.VMEM] * len(args)
    outs = outs or [pltpu.VMEM] * len(shapes)
    return pl.pallas_call(
        body,
        out_shape=[
            jax.ShapeDtypeStruct(s, t) for s, t in zip(shapes, types or [F32] * len(shapes))
        ],
        in_specs=[pl.BlockSpec(memory_space=m) for m in ins],
        out_specs=[pl.BlockSpec(memory_space=m) for m in outs],
        scratch_shapes=scratch,
        compiler_params=pltpu.CompilerParams(vmem_limit_bytes=limit),
        cost_estimate=cost,
    )(*args)


def local(coeffs, obs_cell, obs_value, obs_count):
    def ring(x, axis, size, step):
        return lax.ppermute(x, axis, [(i, (i + step) % size) for i in range(size)])

    packed, listed, space = call(
        sort_body,
        [(TILES, MESSAGE, 128), (LISTED + 32, 128), (TILES, LISTED, 128)],
        [
            pltpu.VMEM((1, SLOTS), I32),
            pltpu.VMEM((REALS, SLOTS), F32),
            pltpu.VMEM((4, ROWS, COLS), F32),
            pltpu.SemaphoreType.DMA((3,)),
        ],
        obs_count,
        obs_cell.reshape(1, SLOTS),
        obs_value,
        coeffs,
        ins=[pltpu.SMEM, pltpu.HBM, pltpu.HBM, pltpu.HBM],
        outs=[pltpu.VMEM, pltpu.VMEM, pltpu.HBM],
        limit=60 * 1024 * 1024,
    )
    recv = lax.all_to_all(packed, "tile", 0, 0)

    work = [
        pltpu.VMEM((REALS, DENSE), F32),
        pltpu.VMEM((REALS, DENSE), I32),
        pltpu.VMEM((COLS, DENSE), BF16),
        pltpu.VMEM((96, DENSE), BF16),
        pltpu.VMEM((48, COLS), F32),
    ]
    sides = [(72, 128), (72, 128)]
    edge_l, edge_r, flag = call(
        edge_body,
        sides + [(1,)],
        work,
        recv,
        listed,
        outs=[pltpu.VMEM, pltpu.VMEM, pltpu.SMEM],
        types=[F32, F32, I32],
    )

    def share(recv, listed, space, edge_l, edge_r):
        whole = jnp.broadcast_to(listed[None, :LISTED], (TILES, LISTED, 128))
        whole = lax.all_to_all(whole, "tile", 0, 0)
        return (whole, *call(rest_body, sides, work, recv, whole, edge_l, edge_r))

    def skip(recv, listed, space, edge_l, edge_r):
        return space, edge_l, edge_r

    whole, edge_l, edge_r = lax.cond(flag[0] > 0, share, skip, recv, listed, space, edge_l, edge_r)
    b, w = call(
        scatter_body,
        [(EXT, REALS, COLS), (EXT, COLS)],
        [
            pltpu.VMEM((REALS, DENSE), F32),
            pltpu.VMEM((REALS, DENSE), I32),
            pltpu.VMEM((COLS, DENSE), BF16),
            pltpu.VMEM((4, 16 * PIECE + 48, DENSE), BF16),
            pltpu.VMEM((4, 40, COLS), F32),
            pltpu.VMEM((TILES, LISTED, 128), F32),
            pltpu.SemaphoreType.DMA,
        ],
        recv,
        whole,
        ins=[pltpu.VMEM, pltpu.HBM],
        cost=pl.CostEstimate(flops=2 * 2368 * DENSE * COLS, bytes_accessed=1 << 23, transcendentals=0),
    )
    from_l = ring(edge_r, "region", REGIONS, 1)
    from_r = ring(edge_l, "region", REGIONS, -1)
    field = (ROWS, REALS, COLS)
    q, t, moments, own = call(
        krylov_body,
        [field, field, (128, 128), (8, 128)],
        [
            pltpu.VMEM((EXT + 2, REALS, WIDE), F32),
            pltpu.VMEM((EXT, WIDE), F32),
            pltpu.VMEM((4, EXT + 16, WIDE), F32),
            pltpu.VMEM((5, EXT + 2, WIDE), F32),
            pltpu.VMEM((EXT + 2, REALS, WIDE), F32),
            pltpu.VMEM((EXT + 2, REALS, WIDE), F32),
            pltpu.VMEM((72, 128), F32),
            pltpu.VMEM((72, 128), F32),
        ],
        b,
        w,
        coeffs,
        recv,
        from_l,
        from_r,
    )
    shared = lax.all_to_all(moments, ("region", "tile"), 0, 0, tiled=True)
    return tuple(
        call(
            finish_body,
            [field, field],
            [
                pltpu.VMEM(field, F32),
                pltpu.VMEM(field, F32),
                pltpu.SemaphoreType.DMA((2, ROWS // PART)),
            ],
            shared,
            own,
            b,
            q,
            t,
            outs=[pltpu.HBM, pltpu.HBM],
        )
    )


def solution(mesh):
    placed = (
        P(None, "tile", "region"),
        P(("region", "tile")),
        P(None, ("region", "tile")),
        P(("region", "tile")),
    )
    return jax.shard_map(
        local,
        mesh=mesh,
        in_specs=placed,
        out_specs=(P("tile", None, "region"), P("tile", None, "region")),
        check_vma=False,
    )
```
